256 devices in a mesh: section: 4 (over y), depth: 4 (over z_hi), grid: 16 (over z_lo, x, core).
Axes of the slice: x: 4, y: 4, z: 8 (z_hi: 4, z_lo: 2; z = z_hi * 2 + z_lo), core: 2. Of those that a mesh axis runs over, the one named last changes fastest.
Arguments:
- section_input: bfloat16 [4, 1024, 6144], P('section', 'depth', 'grid'), may hold values from -24 to 24
- cotangent: bfloat16 [4, 1024, 6144], P('section', 'depth', 'grid'), may hold values from -1.796875 to 1.796875
- projections: bfloat16 [4, 6144, 4, 4096], P('section', 'depth', None, 'grid'), may hold values from -0.25 to 0.25
- norm_gain: bfloat16 [4, 6144], P('section', 'grid'), may hold values from 0.099609375 to 1.8984375
- head_gains: bfloat16 [4, 2, 32, 128], P('section', None, 'grid'), may hold values from 0.099609375 to 1.8984375
Outputs:
- next_branch: bfloat16 [4, 1024, 6144], P('section', 'depth', 'grid')
- returned_grad: bfloat16 [4, 1024, 6144], P('section', 'depth', 'grid')
- projection_grad: bfloat16 [4, 6144, 4, 4096], P('section', 'depth', None, 'grid')
- norm_gain_grad: float32 [4, 6144], P('section', 'grid')
- head_gain_grad: float32 [4, 2, 32, 128], P('section', None, 'grid')
The draws below stay inside these ranges and needn't reach their ends.
All inputs are finite; a program needn't handle non-finite values.
Results may differ from the reference program's by a relative error of at most 0.025.
Values may be sent and summed in bfloat16 or wider, within the bound.
A program may use at most 128 MiB of HBM per device.

```python
import math
import jax
import jax.numpy as jnp
from jax import lax

D = 6144
HEADS = 32
HD = 128
SEQ = 256
TOKENS = 1024
SECTIONS = 4
N_DEPTH = 4
N_GRID = 16


def draw_section_input(key, part):
    key = jax.random.fold_in(key, 11)
    base_key, row_key, col_key = jax.random.split(key, 3)
    row_scale = jnp.exp(jax.random.uniform(row_key, (SECTIONS, TOKENS, 1), minval=math.log(0.3), maxval=math.log(3.0)))
    col_scale = jnp.exp(jax.random.uniform(col_key, (SECTIONS, 1, D), minval=math.log(0.3), maxval=math.log(3.0)))
    base = jax.random.normal(base_key, (SECTIONS, TOKENS, D))
    values = jnp.clip(base * row_scale * col_scale, -24.0, 24.0)
    return values.astype(jnp.bfloat16)


def level_of(own_key, dims, pieces, smallest, top_value):
    factor_of, own = 1.0, jax.random.fold_in(own_key, 6)
    for dim, parts in pieces:
        steps = jnp.exp(jax.random.uniform(jax.random.fold_in(own, dim), (parts,), jnp.float32, smallest / len(pieces), top_value / len(pieces)))
        factor_of = factor_of * jnp.repeat(steps, dims[dim] // parts).reshape([-1 if axis == dim else 1 for axis in range(len(dims))])
    return factor_of


def bell_draw(rng, shape, width, reach, cuts=(), dtype=jnp.bfloat16):
    level = level_of(rng, shape, cuts, -0.22, 0.18) if cuts else 1.0
    values = jax.random.normal(rng, shape, jnp.float32) * width * level
    return jnp.minimum(jnp.maximum(values, -reach), reach).astype(dtype)


def setup_inputs(seed: int = 0) -> dict:
    key_of = jax.random.split(jax.random.key(seed), 6)
    section_input = draw_section_input(jax.random.fold_in(key_of[5], 71), 0)
    cotangent = bell_draw(key_of[1], (SECTIONS, TOKENS, D), 0.3, 1.796875, ((0, 4), (1, 4), (2, 16)))
    projections = bell_draw(key_of[2], (SECTIONS, D, 4, HEADS * HD), ((D * HEADS * HD // 100) ** 0.5) ** -0.5, 0.25, ((0, 4), (1, 4), (3, 16)))
    norm_gain = jnp.clip(1.0 + 0.18 * jax.random.normal(key_of[3], (SECTIONS, D), jnp.float32), 0.099609375, 1.8984375).astype(jnp.bfloat16)
    head_gains = jnp.clip(1.0 + 0.18 * jax.random.normal(key_of[4], (SECTIONS, 2, HEADS, HD), jnp.float32), 0.099609375, 1.8984375).astype(jnp.bfloat16)
    return dict(section_input=section_input, cotangent=cotangent, projections=projections, norm_gain=norm_gain, head_gains=head_gains)


epsilon = 1e-06

def normalize(values):
    centre = lax.optimization_barrier(jnp.mean(values, axis=-1, keepdims=True))
    second = lax.optimization_barrier(jnp.mean(values * values, axis=-1, keepdims=True))
    reciprocal = lax.rsqrt(second - centre * centre + epsilon)
    return ((values - centre) * reciprocal, reciprocal, centre)

def normalize_back(upstream, normed, reciprocal, gain_row):
    scaled = upstream * gain_row
    first_mean = lax.optimization_barrier(jnp.mean(scaled, axis=-1, keepdims=True))
    second_mean = lax.optimization_barrier(jnp.mean(scaled * normed, axis=-1, keepdims=True))
    return reciprocal * (scaled - first_mean - normed * second_mean)

def stored(values):
    return lax.optimization_barrier(values.astype(jnp.bfloat16))

def group_terms(left_side, right_side, groups):
    stride = left_side.shape[1] // groups
    running = jnp.zeros((left_side.shape[0], right_side.shape[0]), jnp.float32)
    for group_index in range(groups):
        lower_col = group_index * stride
        partial_sum = jnp.dot(left_side[:, lower_col:lower_col + stride], right_side[:, lower_col:lower_col + stride].T, preferred_element_type=jnp.float32)
        running = running + stored(partial_sum).astype(jnp.float32)
    return running

def one_section(inputs, upstream, weights, norm_gain, head_gains):
    inner = HEADS * HD
    images = TOKENS // SEQ
    centred, reciprocal, centre = normalize(inputs.astype(jnp.float32))
    normed = stored(centred * norm_gain.astype(jnp.float32))
    projected = jnp.dot(normed, weights[:, :3].reshape(D, 3 * inner), preferred_element_type=jnp.float32)
    projected = projected.reshape(TOKENS, 3, HEADS, HD)
    gains = head_gains.astype(jnp.float32)
    query_parts = normalize(projected[:, 0])
    key_parts = normalize(projected[:, 1])
    query_hat, query_rec = (query_parts[0], query_parts[1])
    key_hat, key_rec = (key_parts[0], key_parts[1])
    query_low = stored(query_hat * gains[0])
    key_low = stored(key_hat * gains[1])
    value_low = stored(projected[:, 2])
    score_scale = HD ** (-0.5)

    def by_image(tensor):
        return tensor.astype(jnp.float32).reshape(images, SEQ, HEADS, HD)
    scores = jnp.einsum('ishd,ijhd->ihsj', by_image(query_low), by_image(key_low)) * score_scale
    exponent = jnp.exp(scores)
    attention = exponent / lax.optimization_barrier(jnp.sum(exponent, axis=-1, keepdims=True))
    attention_low = stored(attention).astype(jnp.float32)
    attended = stored(jnp.einsum('ihsj,ijhd->ishd', attention_low, by_image(value_low))).reshape(TOKENS, inner)
    out_weight = weights[:, 3]
    branch = group_terms(attended, out_weight, N_GRID).astype(jnp.bfloat16)
    d_attended = stored(jnp.dot(upstream, out_weight, preferred_element_type=jnp.float32))
    d_image = by_image(d_attended)
    d_attention = jnp.einsum('ishd,ijhd->ihsj', d_image, by_image(value_low))
    row_delta = lax.optimization_barrier(jnp.sum(attention * d_attention, axis=-1, keepdims=True))
    d_score = stored(attention * (d_attention - row_delta) * score_scale).astype(jnp.float32)
    d_query = jnp.einsum('ihsj,ijhd->ishd', d_score, by_image(key_low)).reshape(TOKENS, HEADS, HD)
    d_key = jnp.einsum('ihsj,ishd->ijhd', d_score, by_image(query_low)).reshape(TOKENS, HEADS, HD)
    d_value = stored(jnp.einsum('ihsj,ishd->ijhd', attention_low, d_image)).reshape(TOKENS, HEADS, HD)
    grad_query = stored(normalize_back(d_query, query_hat, query_rec, gains[0]))
    grad_key = stored(normalize_back(d_key, key_hat, key_rec, gains[1]))
    d_project = jnp.stack([grad_query, grad_key, d_value], axis=1).reshape(TOKENS, 3, inner)
    group_width = inner // N_GRID
    left_side = d_project.reshape(TOKENS, 3, N_GRID, group_width).transpose(0, 2, 1, 3).reshape(TOKENS, 3 * inner)
    right_side = weights[:, :3].reshape(D, 3, N_GRID, group_width).transpose(0, 2, 1, 3).reshape(D, 3 * inner)
    d_normed = group_terms(left_side, right_side, N_GRID)
    weighted = d_normed * norm_gain.astype(jnp.float32)
    first_mean = lax.optimization_barrier(jnp.mean(weighted, axis=-1, keepdims=True))
    second_mean = lax.optimization_barrier(jnp.mean(weighted * centred, axis=-1, keepdims=True))
    input_grad = (reciprocal * (weighted - first_mean - centred * second_mean)).astype(jnp.bfloat16)
    qkv_grad = group_terms(normed.T, d_project.reshape(TOKENS, 3 * inner).T, N_DEPTH).reshape(D, 3, inner)
    out_grad = group_terms(upstream.T, attended.T, N_DEPTH)
    projection_grad = jnp.concatenate([qkv_grad, out_grad[:, None]], axis=1).astype(jnp.bfloat16)
    norm_gain_grad = lax.optimization_barrier(jnp.sum(d_normed * centred, axis=0))
    head_gain_grad = jnp.stack([lax.optimization_barrier(jnp.sum(d_query * query_hat, axis=0)), lax.optimization_barrier(jnp.sum(d_key * key_hat, axis=0))])
    return (branch, input_grad, projection_grad, norm_gain_grad, head_gain_grad)

def reference(section_input, cotangent, projections, norm_gain, head_gains):
    results = [one_section(section_input[section_index], cotangent[section_index], projections[section_index], norm_gain[section_index], head_gains[section_index]) for section_index in range(SECTIONS)]
    branches = jnp.stack([entry[0] for entry in results])
    input_grads = jnp.stack([entry[1] for entry in results])
    weight_grads = jnp.stack([entry[2] for entry in results])
    gain_grads = jnp.stack([entry[3] for entry in results])
    head_grads = jnp.stack([entry[4] for entry in results])
    return (jnp.roll(branches, 1, axis=0), jnp.roll(input_grads, -1, axis=0), weight_grads, gain_grads, head_grads)
```

```python
from types import SimpleNamespace

import jax
import jax.numpy as jnp
from jax import lax
from jax.experimental import pallas as pl
from jax.experimental.pallas import tpu as pltpu
from jax.sharding import PartitionSpec as P

SEQ = 256
HALF = 128
QUARTER = 64
EPSILON = 1e-06
MESH = pl.DeviceIdType.MESH
BF16 = jnp.bfloat16
F32 = jnp.float32
FEATURES = 384
ROWS = 1536
HEAD = 128
QKV = 768
COLS = 1024
GRID = 16
SCALE = HEAD ** (-0.5)


def remote(src, dst, send_sem, recv_sem, device):
    return pltpu.make_async_remote_copy(
        src_ref=src,
        dst_ref=dst,
        send_sem=send_sem,
        recv_sem=recv_sem,
        device_id=device,
        device_id_type=MESH,
    )


def normalize(values):
    centre = jnp.mean(values, axis=-1, keepdims=True)
    second = jnp.mean(values * values, axis=-1, keepdims=True)
    reciprocal = lax.rsqrt(second - centre * centre + EPSILON)
    return (values - centre) * reciprocal, reciprocal


def normalize_back(upstream, normed, reciprocal, gain_row):
    scaled = upstream * gain_row
    first_mean = jnp.mean(scaled, axis=-1, keepdims=True)
    second_mean = jnp.mean(scaled * normed, axis=-1, keepdims=True)
    return reciprocal * (scaled - first_mean - normed * second_mean)


def dot(a, b):
    return jnp.dot(a, b, preferred_element_type=F32)


def dot_nt(a, b):
    return lax.dot_general(a, b, (((1,), (1,)), ((), ())), preferred_element_type=F32)


def dot_tn(a, b):
    return lax.dot_general(a, b, (((0,), (0,)), ((), ())), preferred_element_type=F32)


def vmem(shape, dtype):
    return pltpu.VMEM(shape, dtype)


def dma(count):
    return pltpu.SemaphoreType.DMA((count,))


def gather_scratch():
    return dict(
        own_send=dma(4),
        near_recv=dma(4),
        side_send=dma(8),
        side_recv=dma(8),
        far_send=dma(8),
        far_recv=dma(8),
        sib_send=dma(16),
        sib_recv=dma(16),
        half_send=dma(2),
        half_recv=dma(2),
        full_send=dma(4),
        full_recv=dma(4),
        ring_send=dma(6),
        ring_recv=dma(6),
    )


def reduce_scratch():
    return dict(
        sib_out=vmem((8, SEQ, FEATURES), BF16),
        sib_in=vmem((8, SEQ, FEATURES), BF16),
        keep=vmem((8, SEQ, FEATURES), F32),
        far_out=vmem((8, QUARTER, FEATURES), BF16),
        far_in=vmem((8, QUARTER, FEATURES), BF16),
        side_out=vmem((8, HALF, FEATURES), BF16),
        side_in=vmem((8, HALF, FEATURES), BF16),
        total=vmem((4, HALF, FEATURES), F32),
        next_out=vmem((4, HALF, FEATURES), BF16),
        mate_in=vmem((4, HALF, FEATURES), BF16),
        last_in=vmem((4, HALF, FEATURES), BF16),
        r_sib_send=dma(8),
        r_sib_recv=dma(8),
        r_far_send=dma(8),
        r_far_recv=dma(8),
        r_side_send=dma(8),
        r_side_recv=dma(8),
        r_next_send=dma(4),
        r_mate_recv=dma(4),
        r_last_recv=dma(4),
    )


def sum_scratch(count, rows, columns):
    return dict(
        out=vmem((rows, columns), F32),
        slots=vmem((count, rows, columns), F32),
        send=dma(count),
        recv=dma(count),
    )


SCRATCH = dict(
    acts=gather_scratch(),
    cots=gather_scratch(),
    branch=reduce_scratch(),
    inputs=reduce_scratch(),
    stat_a=sum_scratch(GRID, 8, SEQ),
    stat_b=sum_scratch(GRID, 8, SEQ),
    gains=sum_scratch(4, 8, HEAD),
    norms=sum_scratch(4, 8, FEATURES),
    sems=dict(w=dma(1), grad_send=dma(1), grad_recv=dma(1)),
    buf=dict(
        w=vmem((ROWS, COLS), BF16),
        norm=vmem((SEQ, FEATURES), BF16),
        centred=vmem((SEQ, FEATURES), F32),
        recip=vmem((SEQ, HEAD), F32),
        big_x=vmem((4 * SEQ, ROWS), BF16),
        big_c=vmem((4 * SEQ, ROWS), BF16),
        far_out=vmem((SEQ, COLS), BF16),
        up_out=vmem((SEQ, COLS), BF16),
        down_out=vmem((SEQ, COLS), BF16),
        half_minus=vmem((SEQ, COLS), BF16),
        half_plus=vmem((SEQ, COLS), BF16),
        full_minus=vmem((SEQ, COLS), BF16),
        full_plus=vmem((SEQ, COLS), BF16),
        up_acc=vmem((SEQ, COLS), F32),
        down_acc=vmem((SEQ, COLS), F32),
        own_acc=vmem((SEQ, COLS), F32),
        attention=vmem((2, SEQ, SEQ), F32),
        hats=vmem((4, SEQ, HEAD), F32),
        recs=vmem((4, SEQ, HEAD), F32),
        lows=vmem((6, SEQ, HEAD), BF16),
        att=vmem((4 * SEQ, 256), BF16),
        dp=vmem((4 * SEQ, QKV), BF16),
        grad_out=vmem((SEQ, FEATURES), BF16),
        grad_in=vmem((SEQ, FEATURES), BF16),
    ),
)
LEAVES, TREE = jax.tree.flatten(SCRATCH)


def kernel(*refs):
    x_ref, cot_ref, w_hbm, ng_ref, hg_ref = refs[:5]
    nb_ref, rg_ref, dw_ref, ngg_ref, hgg_ref = refs[5:10]
    parts = jax.tree.unflatten(TREE, refs[10:])
    parts = {name: SimpleNamespace(**part) for name, part in parts.items()}
    acts, cots, branch, inputs = (parts[name] for name in ("acts", "cots", "branch", "inputs"))
    stat_a, stat_b, gains, norms = (parts[name] for name in ("stat_a", "stat_b", "gains", "norms"))
    sems, buf = parts["sems"], parts["buf"]
    w = buf.w

    s = lax.axis_index("section")
    d = lax.axis_index("depth")
    g = lax.axis_index("grid")
    z = g // 8
    x = (g // 2) % 4
    c = g % 2
    base = 2 * (d % 2)
    place = (x - base + 4) % 4
    up = (d + 1) % 4
    down = (d + 3) % 4
    across = (d + 2) % 4

    def at(depth, z_, x_, c_, section=None):
        return (s if section is None else section, depth, z_ * 8 + x_ * 2 + c_)

    sibling = at(d, z, x, 1 - c)
    left_x = (x + 3) % 4
    right_x = (x + 1) % 4
    places = (x, left_x, right_x, (x + 2) % 4)
    left = at(d, z, left_x, c)
    right = at(d, z, right_x, c)
    above = at(up, z, x, c)
    below = at(down, z, x, c)
    section_up = (s + 1) % 4
    section_down = (s + 3) % 4
    home = g // 4
    home_block = g % 4
    home_base = 2 * (home % 2)
    home_other = (home_base + 3 - (x - home_base + 4) % 4) % 4
    owner_x = base + ((place + 1) // 2) % 2
    mate = at(d, 1 - z, x, c)

    def entry(t, depth):
        k = (t - depth + 4) % 4
        middle = depth // 2
        return (k % 2) * ((3 - k) // 2) + (1 - k % 2) * (middle + (k // 2) * (1 - 2 * middle))


    barrier = pltpu.get_barrier_semaphore()

    def greet(device):
        pl.semaphore_signal(barrier, inc=1, device_id=device, device_id_type=MESH)

    for k in range(1, GRID):
        greet((s, d, (g + k) % GRID))
    for k in range(1, 4):
        greet(at((d + k) % 4, z, x, c))
        greet(at((d + k) % 4, d // 2, owner_x, c))
    greet((section_up, d, g))
    for zz in range(2):
        for xx in (x, home_other):
            greet(at(home, zz, xx, c, section_down))

    @pl.when(home != d)
    def _():
        for zz in range(2):
            for xx in (x, home_other):
                greet(at(home, zz, xx, c))

    pl.semaphore_wait(barrier, 26 + 4 * (((home - d + 4) % 4 + 3) // 4))

    w_copy = pltpu.make_async_copy(w_hbm, w, sems.w.at[0])
    w_copy.start()

    def tokens(t):
        return pl.ds(pl.multiple_of(t * SEQ, SEQ), SEQ)

    def features(j):
        return pl.ds(pl.multiple_of(j * FEATURES, FEATURES), FEATURES)

    def own_copy(src, big, kind, h, zz):
        rows = pl.ds(pl.multiple_of(d * SEQ + h * HALF, HALF), HALF)
        return remote(
            src.at[h * HALF : (h + 1) * HALF, :],
            big.at[rows, features(home_block)],
            kind.own_send.at[2 * h + zz],
            kind.near_recv.at[d],
            at(home, zz, home_other if h else x, c),
        )

    def own_send(src, big, kind):
        for zz in range(2):
            here = jnp.logical_and(home == d, z == zz)

            @pl.when(here)
            def _():
                pltpu.make_async_copy(
                    src.at[0:HALF, :],
                    big.at[pl.ds(pl.multiple_of(d * SEQ, SEQ), HALF), features(home_block)],
                    kind.near_recv.at[d],
                ).start()

            @pl.when(jnp.logical_not(here))
            def _():
                own_copy(src, big, kind, 0, zz).start()

            own_copy(src, big, kind, 1, zz).start()

    def block(big, t, x_, c_, lo=0, count=HALF):
        p = (x_ - base + 4) % 4
        start = pl.multiple_of(t * SEQ + (p // 2) * HALF + lo, QUARTER)
        return big.at[pl.ds(start, count), features(2 * (((p + 1) // 2) % 2) + c_)]

    def side_copy(big, kind, t, side, arriving=False):
        ref = block(big, t, places[1 + side] if arriving else x, c)
        slot = 2 * t + side
        return remote(
            ref, ref, kind.side_send.at[slot], kind.side_recv.at[slot], (right, left)[side]
        )

    def far_copy(big, kind, t, side, arriving=False):
        ref = block(big, t, places[3 if arriving else 1 + side], c, side * QUARTER, QUARTER)
        slot = 2 * t + side
        return remote(
            ref, ref, kind.far_send.at[slot], kind.far_recv.at[slot], (right, left)[side]
        )

    def sib_copy(big, kind, t, part, arriving=False):
        ref = block(big, t, places[part], 1 - c if arriving else c)
        slot = 4 * t + part
        return remote(ref, ref, kind.sib_send.at[slot], kind.sib_recv.at[slot], sibling)

    def near_step(big, kind, t):
        ref = block(big, t, x, c)
        remote(ref, ref, kind.side_send.at[2 * t], kind.near_recv.at[t], right).wait_recv()
        side_copy(big, kind, t, 0).start()
        side_copy(big, kind, t, 1).start()
        sib_copy(big, kind, t, 0).start()

    def side_sent(big, kind, t):
        side_copy(big, kind, t, 0).wait_send()
        side_copy(big, kind, t, 1).wait_send()

    def side_step(big, kind, t):
        for side in range(2):
            side_copy(big, kind, t, side, True).wait_recv()
            far_copy(big, kind, t, side).start()
            sib_copy(big, kind, t, 1 + side).start()

    def far_step(big, kind, t):
        far_copy(big, kind, t, 0, True).wait_recv()
        far_copy(big, kind, t, 1, True).wait_recv()
        sib_copy(big, kind, t, 3).start()

    def sib_step(big, kind, t):
        for part in range(4):
            sib_copy(big, kind, t, part, True).wait_recv()

    def drain_gather(src, big, kind):
        for zz in range(2):

            @pl.when(jnp.logical_or(home != d, z != zz))
            def _():
                own_copy(src, big, kind, 0, zz).wait_send()

            own_copy(src, big, kind, 1, zz).wait_send()
        for t in range(4):
            for part in range(4):
                sib_copy(big, kind, t, part).wait_send()
            far_copy(big, kind, t, 0).wait_send()
            far_copy(big, kind, t, 1).wait_send()

    def half_copy(kind, lo, count, side):
        cut = lo + side * (count // 2)
        cols = slice(cut, cut + count // 2)
        dst = buf.half_minus if side == 0 else buf.half_plus
        return remote(
            buf.far_out.at[:, cols],
            dst.at[:, cols],
            kind.half_send.at[side],
            kind.half_recv.at[side],
            above if side == 0 else below,
        )

    def full_copy(kind, lo, count, side, part):
        cut = lo + part * (count // 2)
        cols = slice(cut, cut + count // 2)
        src = buf.up_out if side == 0 else buf.down_out
        dst = buf.full_minus if side == 0 else buf.full_plus
        return remote(
            src.at[:, cols],
            dst.at[:, cols],
            kind.full_send.at[2 * side + part],
            kind.full_recv.at[2 * side + part],
            above if side == 0 else below,
        )

    def pass_on(kind, lo, count, side, part):
        acc = buf.up_acc if side == 0 else buf.down_acc
        out = buf.up_out if side == 0 else buf.down_out
        got = buf.half_minus if side == 0 else buf.half_plus
        cut = lo + part * (count // 2)
        cols = slice(cut, cut + count // 2)
        value = acc[:, cols]
        if part == side:
            half_copy(kind, lo, count, side).wait_recv()
            value = value + got[:, cols].astype(F32)
        out[:, cols] = value.astype(BF16)
        full_copy(kind, lo, count, side, part).start()

    def multiply(big, kind, lo, count, t, ref):
        sib_step(big, kind, t)
        for q in range(lo, lo + count, 256):
            ref[:, q : q + 256] = dot(big[tokens(t), :], w[:, q : q + 256]).astype(ref.dtype)

    def multiply_step(big, kind, lo, count, r):
        if r == 0:
            multiply(big, kind, lo, count, d, buf.own_acc)
        elif r == 1:
            multiply(big, kind, lo, count, up, buf.up_acc)
            pass_on(kind, lo, count, 0, 1)
        elif r == 3:
            multiply(big, kind, lo, count, down, buf.down_acc)
            pass_on(kind, lo, count, 1, 0)
        else:
            multiply(big, kind, lo, count, across, buf.far_out)
            half_copy(kind, lo, count, 0).start()
            half_copy(kind, lo, count, 1).start()

    def finish_depth(kind, lo, count):
        cols = slice(lo, lo + count)
        for side in range(2):
            full_copy(kind, lo, count, side, 0).wait_recv()
            full_copy(kind, lo, count, side, 1).wait_recv()
        buf.own_acc[:, cols] = (
            buf.own_acc[:, cols]
            + buf.full_minus[:, cols].astype(F32)
            + buf.full_plus[:, cols].astype(F32)
        )

    def drain_depth(kind, lo, count):
        for side in range(2):
            half_copy(kind, lo, count, side).wait_send()
            full_copy(kind, lo, count, side, 0).wait_send()
            full_copy(kind, lo, count, side, 1).wait_send()

    def ring_block(ref, step, t):
        half = ref.shape[1] // 2
        second = step in (1, 2, 5)
        return ref.at[tokens(t), half:] if second else ref.at[tokens(t), :half]

    def ring_copy(ref, kind, step):
        block = ring_block(ref, step, (d, d, d, d, down, up)[step])
        return remote(
            block,
            block,
            kind.ring_send.at[step],
            kind.ring_recv.at[step],
            above if step % 2 == 0 else below,
        )

    def ring_wait(ref, kind, step):
        block = ring_block(ref, step, (down, up, down, up, across, across)[step])
        remote(
            block,
            block,
            kind.ring_send.at[step],
            kind.ring_recv.at[step],
            above if step % 2 == 0 else below,
        ).wait_recv()

    def ring_start(ref, kind):
        ring_copy(ref, kind, 0).start()
        ring_copy(ref, kind, 1).start()

    def ring_more(ref, kind):
        for step in range(2):
            ring_copy(ref, kind, step).wait_send()
            ring_copy(ref, kind, step + 2).start()

    def ring_forward(ref, kind):
        for step in range(2):
            ring_wait(ref, kind, step)
            ring_copy(ref, kind, step + 2).wait_send()
            ring_copy(ref, kind, step + 4).start()

    def ring_near(ref, kind):
        ring_wait(ref, kind, 2)
        ring_wait(ref, kind, 3)

    def ring_far(ref, kind):
        ring_wait(ref, kind, 4)
        ring_wait(ref, kind, 5)

    def r_sib(kind, t, i):
        slot = 2 * t + i
        return remote(
            kind.sib_out.at[slot],
            kind.sib_in.at[slot],
            kind.r_sib_send.at[slot],
            kind.r_sib_recv.at[slot],
            sibling,
        )

    def r_far(kind, t, side):
        slot = 2 * t + side
        return remote(
            kind.far_out.at[slot],
            kind.far_in.at[slot],
            kind.r_far_send.at[slot],
            kind.r_far_recv.at[slot],
            (right, left)[side],
        )

    def r_side(kind, t, side):
        slot = 2 * t + side
        return remote(
            kind.side_out.at[slot],
            kind.side_in.at[slot],
            kind.r_side_send.at[slot],
            kind.r_side_recv.at[slot],
            (right, left)[side],
        )

    def r_mate(kind, t):
        return remote(
            kind.next_out.at[t],
            kind.mate_in.at[t],
            kind.r_next_send.at[t],
            kind.r_mate_recv.at[t],
            mate,
        )

    def r_last(kind, t, act):
        slot = place // 2 if kind is branch else 2 * (place // 2) + z
        dst = kind.last_in.at[slot]
        recv = kind.r_last_recv.at[slot]
        src = kind.next_out.at[t]
        section = section_up if kind is branch else s
        copy = remote(src, dst, kind.r_next_send.at[t], recv, at(t, d // 2, owner_x, c, section))

        def away():
            if act == "start":
                copy.start()
            else:
                copy.wait_send()

        if kind is branch:
            away()
        else:
            here = jnp.logical_and(t == d, jnp.logical_and(place < 2, z == d // 2))
            pl.when(jnp.logical_not(here))(away)

            @pl.when(here)
            def _():
                if act == "start":
                    pltpu.make_async_copy(src, dst, recv).start()

    def total_of(kind, t, x_, lo, count):
        p = (x_ - base + 4) % 4
        slot = 2 * t + ((p + 1) // 2) % 2
        rows = pl.ds(pl.multiple_of((p // 2) * HALF + lo, QUARTER), count)
        return kind.keep[slot, rows, :] + kind.sib_in[slot, rows, :].astype(F32)

    def first_stage(ref, kind, lo, t):
        count = ref.shape[1]
        left = ref[tokens(t), :]
        for i in range(2):
            rows = features(2 * i + 1 - c)
            value = dot_nt(left, w[rows, lo : lo + count])
            kind.sib_out[2 * t + i] = value.astype(BF16)
            r_sib(kind, t, i).start()
        for i in range(2):
            rows = features(2 * i + c)
            kind.keep[2 * t + i] = dot_nt(left, w[rows, lo : lo + count])

    def second_stage(kind, t):
        r_sib(kind, t, 0).wait_recv()
        r_sib(kind, t, 1).wait_recv()
        for side in range(2):
            value = total_of(kind, t, places[3], side * QUARTER, QUARTER)
            kind.far_out[2 * t + side] = value.astype(BF16)
            r_far(kind, t, side).start()

    def third_stage(kind, t):
        for side in range(2):
            slot = 2 * t + side
            r_far(kind, t, side).wait_recv()
            for part in range(2):
                value = total_of(kind, t, places[2 - side], part * QUARTER, QUARTER)
                if part == side:
                    value = value + kind.far_in[slot].astype(F32)
                kind.side_out[slot, part * QUARTER : (part + 1) * QUARTER, :] = value.astype(BF16)
            r_side(kind, t, side).start()

    def side_done(kind, t):
        r_side(kind, t, 0).wait_send()
        r_side(kind, t, 1).wait_send()

    def fourth_stage(kind, t):
        r_side(kind, t, 0).wait_recv()
        r_side(kind, t, 1).wait_recv()
        total = total_of(kind, t, x, 0, HALF)
        total = total + kind.side_in[2 * t].astype(F32) + kind.side_in[2 * t + 1].astype(F32)
        if kind is inputs:
            kind.next_out[t] = total.astype(BF16)
            r_last(kind, t, "start")
            return
        kind.total[t] = total

        @pl.when(z != entry(t, d))
        def _():
            kind.next_out[t] = total.astype(BF16)
            r_mate(kind, t).start()

    def fifth_stage(kind, t):
        @pl.when(z == entry(t, d))
        def _():
            r_mate(kind, t).wait_recv()
            total = kind.total[t] + kind.mate_in[t].astype(F32)
            kind.next_out[t] = total.astype(BF16)
            r_last(kind, t, "start")

    def last_stage(kind):
        count = 2 if kind is branch else 4
        for slot in range(count):
            remote(
                kind.last_in.at[slot],
                kind.last_in.at[slot],
                kind.r_next_send.at[0],
                kind.r_last_recv.at[slot],
                sibling,
            ).wait_recv()
        if kind is branch:
            return kind.last_in[0:2].reshape(SEQ, FEATURES).astype(F32)
        halves = [
            kind.last_in[2 * h].astype(F32) + kind.last_in[2 * h + 1].astype(F32) for h in range(2)
        ]
        return jnp.concatenate(halves, axis=0)

    def drain_reduce(kind):
        for t in range(4):
            r_sib(kind, t, 0).wait_send()
            r_sib(kind, t, 1).wait_send()
            r_far(kind, t, 0).wait_send()
            r_far(kind, t, 1).wait_send()

            if kind is inputs:
                r_last(kind, t, "wait")
                continue

            @pl.when(z != entry(t, d))
            def _():
                r_mate(kind, t).wait_send()

            @pl.when(z == entry(t, d))
            def _():
                r_last(kind, t, "wait")

    def stat_copy(name, k):
        return remote(
            name.out,
            name.slots.at[g],
            name.send.at[k],
            name.recv.at[k],
            (s, d, (g + k) % GRID),
        )

    lane = lax.broadcasted_iota(jnp.int32, (SEQ, HEAD), 1)

    def stat_start(name, first, second):
        both = jnp.where(lane == 0, first, jnp.where(lane == 1, second, 0.0))
        turned = both.T[0:8]
        name.out[...] = turned
        name.slots[g] = turned
        for k in range(1, GRID):
            stat_copy(name, k).start()

    def stat_finish(name):
        slots = name.slots
        for k in range(1, GRID):
            slot = slots.at[(g + GRID - k) % GRID]
            remote(
                slot, slot, name.send.at[k], name.recv.at[k], sibling
            ).wait_recv()
        total = jnp.sum(slots[...], axis=0)
        padded = jnp.concatenate([total, jnp.zeros((HEAD - 8, SEQ), F32)], axis=0)
        columns = padded.T
        return columns[:, 0:1], columns[:, 1:2]

    def stat_drain(name):
        for k in range(1, GRID):
            stat_copy(name, k).wait_send()

    def small_copy(name, k):
        return remote(
            name.out,
            name.slots.at[d],
            name.send.at[k],
            name.recv.at[k],
            at((d + k) % 4, z, x, c),
        )

    def small_start(name):
        name.slots[d] = name.out[...]
        for k in range(1, 4):
            small_copy(name, k).start()

    def small_finish(name):
        slots = name.slots
        for k in range(1, 4):
            slot = slots.at[(d + 4 - k) % 4]
            remote(
                slot, slot, name.send.at[k], name.recv.at[k], above
            ).wait_recv()
        return jnp.sum(slots[...], axis=0)

    def small_drain(name):
        for k in range(1, 4):
            small_copy(name, k).wait_send()

    xs = (buf.big_x, acts)
    cs = (buf.big_c, cots)
    xw = (0, QKV)
    cw = (QKV, 256)
    own_send(cot_ref.at[0], buf.big_c, cots)
    values = x_ref[0].astype(F32)
    stat_start(
        stat_a,
        jnp.sum(values, axis=-1, keepdims=True),
        jnp.sum(values * values, axis=-1, keepdims=True),
    )
    first, second = stat_finish(stat_a)
    width = 4 * ROWS
    centre = first / width
    reciprocal = lax.rsqrt(second / width - centre * centre + EPSILON)
    gain = ng_ref[...].astype(F32)
    centred = (x_ref[0].astype(F32) - centre) * reciprocal
    buf.centred[...] = centred
    buf.recip[...] = jnp.broadcast_to(reciprocal, (SEQ, HEAD))
    buf.norm[...] = (centred * gain).astype(BF16)
    near_step(*cs, up)
    near_step(*cs, down)
    near_step(*cs, across)
    near_step(*cs, d)
    own_send(buf.norm, buf.big_x, acts)
    side_step(*cs, up)
    side_step(*cs, down)
    far_step(*cs, up)
    near_step(*xs, across)
    far_step(*cs, down)
    side_step(*cs, across)
    w_copy.wait()
    multiply_step(*cs, *cw, 1)
    far_step(*cs, across)
    side_step(*xs, across)
    multiply_step(*cs, *cw, 3)
    multiply_step(*cs, *cw, 2)
    side_step(*cs, d)
    near_step(*xs, up)
    far_step(*xs, across)
    near_step(*xs, down)
    multiply_step(*xs, *xw, 2)
    side_sent(*cs, down)
    side_step(*xs, down)
    pass_on(cots, *cw, 0, 0)
    far_step(*cs, d)
    near_step(*xs, d)
    side_step(*xs, up)
    pass_on(cots, *cw, 1, 1)
    multiply_step(*cs, *cw, 0)
    far_step(*xs, down)
    multiply_step(*xs, *xw, 3)
    far_step(*xs, up)
    multiply_step(*xs, *xw, 1)
    side_step(*xs, d)
    pass_on(acts, *xw, 0, 0)
    pass_on(acts, *xw, 1, 1)
    far_step(*xs, d)
    side_sent(*cs, across)
    multiply_step(*xs, *xw, 0)
    finish_depth(cots, *cw)
    finish_depth(acts, *xw)
    own = buf.own_acc
    for h in range(2):
        cols = [slice(part * 256 + h * HEAD, part * 256 + (h + 1) * HEAD) for part in range(4)]
        for part in range(2):
            hat, rec = normalize(own[:, cols[part]])
            buf.hats[2 * part + h] = hat
            buf.recs[2 * part + h] = jnp.broadcast_to(rec, (SEQ, HEAD))
            row = hg_ref[0, part, h : h + 1, :].astype(F32)
            buf.lows[2 * part + h] = (hat * row).astype(BF16)
        buf.lows[4 + h] = own[:, cols[2]].astype(BF16)
        scores = dot_nt(buf.lows[h], buf.lows[2 + h]) * SCALE
        exponent = jnp.exp(scores)
        attention = exponent / jnp.sum(exponent, axis=-1, keepdims=True)
        buf.attention[h] = attention
        attended = dot(attention.astype(BF16), buf.lows[4 + h])
        buf.att[tokens(d), h * HEAD : (h + 1) * HEAD] = attended.astype(BF16)
    gains.out[...] = jnp.zeros((8, HEAD), F32)
    for h in range(2):
        d_attended = own[:, QKV + h * HEAD : QKV + (h + 1) * HEAD].astype(BF16)
        attention = buf.attention[h]
        d_attention = dot_nt(d_attended, buf.lows[4 + h])
        row_delta = jnp.sum(attention * d_attention, axis=-1, keepdims=True)
        d_score = (attention * (d_attention - row_delta) * SCALE).astype(BF16)
        d_query = dot(d_score, buf.lows[2 + h])
        d_key = dot_tn(d_score, buf.lows[h])
        d_value = dot_tn(attention.astype(BF16), d_attended)
        for part, upstream in enumerate((d_query, d_key)):
            hat = buf.hats[2 * part + h]
            row = hg_ref[0, part, h : h + 1, :].astype(F32)
            grad = normalize_back(upstream, hat, buf.recs[2 * part + h][:, 0:1], row)
            at_col = part * 256 + h * HEAD
            buf.dp[tokens(d), at_col : at_col + HEAD] = grad.astype(BF16)
            index = 2 * part + h
            gains.out[index : index + 1, :] = jnp.sum(upstream * hat, axis=0, keepdims=True)
        at_col = 512 + h * HEAD
        buf.dp[tokens(d), at_col : at_col + HEAD] = d_value.astype(BF16)
    small_start(gains)
    ring_start(buf.dp, acts)
    ring_start(buf.att, cots)
    first_stage(buf.att, branch, QKV, d)
    ring_more(buf.att, cots)
    second_stage(branch, d)
    ring_forward(buf.att, cots)
    ring_more(buf.dp, acts)
    third_stage(branch, d)
    first_stage(buf.dp, inputs, 0, d)
    ring_near(buf.att, cots)
    first_stage(buf.att, branch, QKV, down)
    first_stage(buf.att, branch, QKV, up)
    ring_far(buf.att, cots)
    side_sent(*xs, up)
    second_stage(branch, up)
    second_stage(inputs, d)
    third_stage(branch, up)
    fourth_stage(branch, d)
    second_stage(branch, down)
    ring_forward(buf.dp, acts)
    first_stage(buf.att, branch, QKV, across)
    second_stage(branch, across)
    third_stage(inputs, d)
    ring_near(buf.dp, acts)
    fourth_stage(branch, up)
    first_stage(buf.dp, inputs, 0, up)
    side_done(inputs, d)
    first_stage(buf.dp, inputs, 0, down)
    third_stage(branch, across)
    side_done(branch, up)
    side_done(branch, across)
    side_sent(*cs, up)
    third_stage(branch, down)
    second_stage(inputs, down)
    second_stage(inputs, up)
    fourth_stage(branch, across)
    ring_far(buf.dp, acts)
    first_stage(buf.dp, inputs, 0, across)
    third_stage(inputs, up)
    fourth_stage(branch, down)
    side_done(branch, down)
    second_stage(inputs, across)
    third_stage(inputs, down)
    fourth_stage(inputs, up)
    side_sent(*cs, d)
    third_stage(inputs, across)
    fourth_stage(inputs, down)
    side_done(inputs, across)
    fourth_stage(inputs, across)
    fourth_stage(inputs, d)
    side_done(branch, d)
    side_done(inputs, down)

    def weight_rows(k, _):
        rows = pl.ds(pl.multiple_of(k * 256, 256), 256)
        dw_ref[rows, 0:QKV] = dot_tn(buf.big_x[:, rows], buf.dp[...]).astype(BF16)
        dw_ref[rows, QKV:COLS] = dot_tn(buf.big_c[:, rows], buf.att[...]).astype(BF16)
        return 0

    lax.fori_loop(0, 6, weight_rows, 0)

    side_sent(*xs, across)
    side_done(inputs, up)
    side_sent(*xs, d)
    d_normed = last_stage(inputs)
    weighted = d_normed * gain
    centred = buf.centred[...]
    stat_start(
        stat_b,
        jnp.sum(weighted, axis=-1, keepdims=True),
        jnp.sum(weighted * centred, axis=-1, keepdims=True),
    )
    norms.out[...] = jnp.broadcast_to(
        jnp.sum(d_normed * centred, axis=0, keepdims=True), (8, FEATURES)
    )
    small_start(norms)
    total = small_finish(gains)
    for part in range(2):
        hgg_ref[0, part] = total[2 * part : 2 * part + 2]
    first, second = stat_finish(stat_b)
    reciprocal = buf.recip[:, 0:1]
    grad = reciprocal * (weighted - first / width - centred * (second / width))
    buf.grad_out[...] = grad.astype(BF16)
    grad_copy = remote(
        buf.grad_out,
        buf.grad_in,
        sems.grad_send.at[0],
        sems.grad_recv.at[0],
        (section_down, d, g),
    )
    grad_copy.start()
    ngg_ref[...] = small_finish(norms)[0:1]
    drain_gather(cot_ref.at[0], buf.big_c, cots)
    drain_gather(buf.norm, buf.big_x, acts)
    drain_depth(acts, 0, QKV)
    drain_depth(cots, QKV, 256)
    for step in range(4, 6):
        ring_copy(buf.att, cots, step).wait_send()
        ring_copy(buf.dp, acts, step).wait_send()
    fifth_stage(branch, across)
    fifth_stage(branch, up)
    side_sent(*xs, down)
    fifth_stage(branch, down)
    fifth_stage(branch, d)
    nb_ref[0] = last_stage(branch).astype(BF16)
    drain_reduce(branch)
    drain_reduce(inputs)
    stat_drain(stat_a)
    stat_drain(stat_b)
    small_drain(gains)
    small_drain(norms)
    grad_copy.wait()
    rg_ref[0] = buf.grad_in[...]


def local(section_input, cotangent, projections, norm_gain, head_gains):
    weights = projections.reshape(ROWS, COLS)
    here = pl.BlockSpec(memory_space=pltpu.VMEM)
    outs = pl.pallas_call(
        kernel,
        out_shape=(
            jax.ShapeDtypeStruct((1, SEQ, FEATURES), BF16),
            jax.ShapeDtypeStruct((1, SEQ, FEATURES), BF16),
            jax.ShapeDtypeStruct((ROWS, COLS), BF16),
            jax.ShapeDtypeStruct((1, FEATURES), F32),
            jax.ShapeDtypeStruct((1, 2, 2, HEAD), F32),
        ),
        in_specs=[here, here, pl.BlockSpec(memory_space=pl.ANY), here, here],
        out_specs=(here,) * 5,
        scratch_shapes=LEAVES,
        compiler_params=pltpu.CompilerParams(
            collective_id=0, has_side_effects=True, vmem_limit_bytes=60 * 1024 * 1024
        ),
        name="block",
    )(section_input, cotangent, weights, norm_gain, head_gains)
    next_branch, returned, weight_grad, norm_total, head_total = outs
    return (
        next_branch,
        returned,
        weight_grad.reshape(1, ROWS, 4, 256),
        norm_total,
        head_total,
    )


def solution(mesh):
    in_specs = (
        P("section", "depth", "grid"),
        P("section", "depth", "grid"),
        P("section", "depth", None, "grid"),
        P("section", "grid"),
        P("section", None, "grid", None),
    )
    out_specs = (
        P("section", "depth", "grid"),
        P("section", "depth", "grid"),
        P("section", "depth", None, "grid"),
        P("section", "grid"),
        P("section", None, "grid", None),
    )
    return jax.shard_map(local, mesh=mesh, in_specs=in_specs, out_specs=out_specs, check_vma=False)
```

```python
from types import SimpleNamespace

import jax
import jax.numpy as jnp
from jax import lax
from jax.experimental import pallas as pl
from jax.experimental.pallas import tpu as pltpu
from jax.sharding import PartitionSpec as P

SEQ = 256
HALF = 128
QUARTER = 64
EPSILON = 1e-06
MESH = pl.DeviceIdType.MESH
BF16 = jnp.bfloat16
F32 = jnp.float32
FEATURES = 384
ROWS = 1536
HEAD = 128
QKV = 768
COLS = 1024
GRID = 16
SCALE = HEAD ** (-0.5)


def remote(src, dst, send_sem, recv_sem, device):
    return pltpu.make_async_remote_copy(
        src_ref=src,
        dst_ref=dst,
        send_sem=send_sem,
        recv_sem=recv_sem,
        device_id=device,
        device_id_type=MESH,
    )


def normalize(values):
    centre = jnp.mean(values, axis=-1, keepdims=True)
    second = jnp.mean(values * values, axis=-1, keepdims=True)
    reciprocal = lax.rsqrt(second - centre * centre + EPSILON)
    return (values - centre) * reciprocal, reciprocal


def normalize_back(upstream, normed, reciprocal, gain_row):
    scaled = upstream * gain_row
    first_mean = jnp.mean(scaled, axis=-1, keepdims=True)
    second_mean = jnp.mean(scaled * normed, axis=-1, keepdims=True)
    return reciprocal * (scaled - first_mean - normed * second_mean)


def dot(a, b):
    return jnp.dot(a, b, preferred_element_type=F32)


def dot_nt(a, b):
    return lax.dot_general(a, b, (((1,), (1,)), ((), ())), preferred_element_type=F32)


def dot_tn(a, b):
    return lax.dot_general(a, b, (((0,), (0,)), ((), ())), preferred_element_type=F32)


def vmem(shape, dtype):
    return pltpu.VMEM(shape, dtype)


def dma(count):
    return pltpu.SemaphoreType.DMA((count,))


def gather_scratch():
    return dict(
        own_send=dma(4),
        near_recv=dma(4),
        side_send=dma(8),
        side_recv=dma(8),
        far_send=dma(8),
        far_recv=dma(8),
        sib_send=dma(16),
        sib_recv=dma(16),
        half_send=dma(2),
        half_recv=dma(2),
        full_send=dma(4),
        full_recv=dma(4),
        ring_send=dma(6),
        ring_recv=dma(6),
    )


def reduce_scratch():
    return dict(
        sib_out=vmem((8, SEQ, FEATURES), BF16),
        sib_in=vmem((8, SEQ, FEATURES), BF16),
        keep=vmem((8, SEQ, FEATURES), F32),
        far_out=vmem((8, QUARTER, FEATURES), BF16),
        far_in=vmem((8, QUARTER, FEATURES), BF16),
        side_out=vmem((8, HALF, FEATURES), BF16),
        side_in=vmem((8, HALF, FEATURES), BF16),
        total=vmem((4, HALF, FEATURES), F32),
        next_out=vmem((4, HALF, FEATURES), BF16),
        mate_in=vmem((4, HALF, FEATURES), BF16),
        last_in=vmem((4, HALF, FEATURES), BF16),
        r_sib_send=dma(8),
        r_sib_recv=dma(8),
        r_far_send=dma(8),
        r_far_recv=dma(8),
        r_side_send=dma(8),
        r_side_recv=dma(8),
        r_next_send=dma(4),
        r_mate_recv=dma(4),
        r_last_recv=dma(4),
    )


def sum_scratch(count, rows, columns):
    return dict(
        out=vmem((rows, columns), F32),
        slots=vmem((count, rows, columns), F32),
        send=dma(count),
        recv=dma(count),
    )


SCRATCH = dict(
    acts=gather_scratch(),
    cots=gather_scratch(),
    branch=reduce_scratch(),
    inputs=reduce_scratch(),
    stat_a=sum_scratch(GRID, 8, SEQ),
    stat_b=sum_scratch(GRID, 8, SEQ),
    gains=sum_scratch(4, 8, HEAD),
    norms=sum_scratch(4, 8, FEATURES),
    sems=dict(w=dma(1), grad_send=dma(1), grad_recv=dma(1)),
    buf=dict(
        w=vmem((ROWS, COLS), BF16),
        raw=vmem((ROWS, 4, 256), BF16),
        norm=vmem((SEQ, FEATURES), BF16),
        centred=vmem((SEQ, FEATURES), F32),
        recip=vmem((SEQ, HEAD), F32),
        big_x=vmem((4 * SEQ, ROWS), BF16),
        big_c=vmem((4 * SEQ, ROWS), BF16),
        far_out=vmem((SEQ, COLS), BF16),
        up_out=vmem((SEQ, COLS), BF16),
        down_out=vmem((SEQ, COLS), BF16),
        half_minus=vmem((SEQ, COLS), BF16),
        half_plus=vmem((SEQ, COLS), BF16),
        full_minus=vmem((SEQ, COLS), BF16),
        full_plus=vmem((SEQ, COLS), BF16),
        up_acc=vmem((SEQ, COLS), F32),
        down_acc=vmem((SEQ, COLS), F32),
        own_acc=vmem((SEQ, COLS), F32),
        attention=vmem((2, SEQ, SEQ), F32),
        hats=vmem((4, SEQ, HEAD), F32),
        recs=vmem((4, SEQ, HEAD), F32),
        lows=vmem((6, SEQ, HEAD), BF16),
        att=vmem((4 * SEQ, 256), BF16),
        dp=vmem((4 * SEQ, QKV), BF16),
        grad_out=vmem((SEQ, FEATURES), BF16),
        grad_in=vmem((SEQ, FEATURES), BF16),
    ),
)
LEAVES, TREE = jax.tree.flatten(SCRATCH)


def kernel(*refs):
    x_ref, cot_ref, w_hbm, ng_ref, hg_ref = refs[:5]
    nb_ref, rg_ref, dw_ref, ngg_ref, hgg_ref = refs[5:10]
    parts = jax.tree.unflatten(TREE, refs[10:])
    parts = {name: SimpleNamespace(**part) for name, part in parts.items()}
    acts, cots, branch, inputs = (parts[name] for name in ("acts", "cots", "branch", "inputs"))
    stat_a, stat_b, gains, norms = (parts[name] for name in ("stat_a", "stat_b", "gains", "norms"))
    sems, buf = parts["sems"], parts["buf"]
    w = buf.w

    s = lax.axis_index("section")
    d = lax.axis_index("depth")
    g = lax.axis_index("grid")
    z = g // 8
    x = (g // 2) % 4
    c = g % 2
    base = 2 * (d % 2)
    place = (x - base + 4) % 4
    up = (d + 1) % 4
    down = (d + 3) % 4
    across = (d + 2) % 4

    def at(depth, z_, x_, c_, section=None):
        return (s if section is None else section, depth, z_ * 8 + x_ * 2 + c_)

    sibling = at(d, z, x, 1 - c)
    left_x = (x + 3) % 4
    right_x = (x + 1) % 4
    places = (x, left_x, right_x, (x + 2) % 4)
    left = at(d, z, left_x, c)
    right = at(d, z, right_x, c)
    above = at(up, z, x, c)
    below = at(down, z, x, c)
    section_up = (s + 1) % 4
    section_down = (s + 3) % 4
    home = g // 4
    home_block = g % 4
    home_base = 2 * (home % 2)
    home_other = (home_base + 3 - (x - home_base + 4) % 4) % 4
    owner_x = base + ((place + 1) // 2) % 2
    mate = at(d, 1 - z, x, c)

    def entry(t, depth):
        k = (t - depth + 4) % 4
        middle = depth // 2
        return (k % 2) * ((3 - k) // 2) + (1 - k % 2) * (middle + (k // 2) * (1 - 2 * middle))


    barrier = pltpu.get_barrier_semaphore()

    def greet(device):
        pl.semaphore_signal(barrier, inc=1, device_id=device, device_id_type=MESH)

    for k in range(1, GRID):
        greet((s, d, (g + k) % GRID))
    for k in range(1, 4):
        greet(at((d + k) % 4, z, x, c))
        greet(at((d + k) % 4, d // 2, owner_x, c))
    greet((section_up, d, g))
    for zz in range(2):
        for xx in (x, home_other):
            greet(at(home, zz, xx, c, section_down))

    @pl.when(home != d)
    def _():
        for zz in range(2):
            for xx in (x, home_other):
                greet(at(home, zz, xx, c))

    pl.semaphore_wait(barrier, 26 + 4 * (((home - d + 4) % 4 + 3) // 4))

    w_copy = pltpu.make_async_copy(w_hbm.at[0], buf.raw, sems.w.at[0])
    w_copy.start()

    def tokens(t):
        return pl.ds(pl.multiple_of(t * SEQ, SEQ), SEQ)

    def features(j):
        return pl.ds(pl.multiple_of(j * FEATURES, FEATURES), FEATURES)

    def own_copy(src, big, kind, h, zz):
        rows = pl.ds(pl.multiple_of(d * SEQ + h * HALF, HALF), HALF)
        return remote(
            src.at[h * HALF : (h + 1) * HALF, :],
            big.at[rows, features(home_block)],
            kind.own_send.at[2 * h + zz],
            kind.near_recv.at[d],
            at(home, zz, home_other if h else x, c),
        )

    def own_send(src, big, kind):
        for zz in range(2):
            here = jnp.logical_and(home == d, z == zz)

            @pl.when(here)
            def _():
                pltpu.make_async_copy(
                    src.at[0:HALF, :],
                    big.at[pl.ds(pl.multiple_of(d * SEQ, SEQ), HALF), features(home_block)],
                    kind.near_recv.at[d],
                ).start()

            @pl.when(jnp.logical_not(here))
            def _():
                own_copy(src, big, kind, 0, zz).start()

            own_copy(src, big, kind, 1, zz).start()

    def block(big, t, x_, c_, lo=0, count=HALF):
        p = (x_ - base + 4) % 4
        start = pl.multiple_of(t * SEQ + (p // 2) * HALF + lo, QUARTER)
        return big.at[pl.ds(start, count), features(2 * (((p + 1) // 2) % 2) + c_)]

    def side_copy(big, kind, t, side, arriving=False):
        ref = block(big, t, places[1 + side] if arriving else x, c)
        slot = 2 * t + side
        return remote(
            ref, ref, kind.side_send.at[slot], kind.side_recv.at[slot], (right, left)[side]
        )

    def far_copy(big, kind, t, side, arriving=False):
        ref = block(big, t, places[3 if arriving else 1 + side], c, side * QUARTER, QUARTER)
        slot = 2 * t + side
        return remote(
            ref, ref, kind.far_send.at[slot], kind.far_recv.at[slot], (right, left)[side]
        )

    def sib_copy(big, kind, t, part, arriving=False):
        ref = block(big, t, places[part], 1 - c if arriving else c)
        slot = 4 * t + part
        return remote(ref, ref, kind.sib_send.at[slot], kind.sib_recv.at[slot], sibling)

    def near_step(big, kind, t):
        ref = block(big, t, x, c)
        remote(ref, ref, kind.side_send.at[2 * t], kind.near_recv.at[t], right).wait_recv()
        side_copy(big, kind, t, 0).start()
        side_copy(big, kind, t, 1).start()
        sib_copy(big, kind, t, 0).start()

    def side_sent(big, kind, t):
        side_copy(big, kind, t, 0).wait_send()
        side_copy(big, kind, t, 1).wait_send()

    def side_step(big, kind, t):
        for side in range(2):
            side_copy(big, kind, t, side, True).wait_recv()
            far_copy(big, kind, t, side).start()
            sib_copy(big, kind, t, 1 + side).start()

    def far_step(big, kind, t):
        far_copy(big, kind, t, 0, True).wait_recv()
        far_copy(big, kind, t, 1, True).wait_recv()
        sib_copy(big, kind, t, 3).start()

    def sib_step(big, kind, t):
        for part in range(4):
            sib_copy(big, kind, t, part, True).wait_recv()

    def drain_gather(src, big, kind):
        for zz in range(2):

            @pl.when(jnp.logical_or(home != d, z != zz))
            def _():
                own_copy(src, big, kind, 0, zz).wait_send()

            own_copy(src, big, kind, 1, zz).wait_send()
        for t in range(4):
            for part in range(4):
                sib_copy(big, kind, t, part).wait_send()
            far_copy(big, kind, t, 0).wait_send()
            far_copy(big, kind, t, 1).wait_send()

    def half_copy(kind, lo, count, side):
        cut = lo + side * (count // 2)
        cols = slice(cut, cut + count // 2)
        dst = buf.half_minus if side == 0 else buf.half_plus
        return remote(
            buf.far_out.at[:, cols],
            dst.at[:, cols],
            kind.half_send.at[side],
            kind.half_recv.at[side],
            above if side == 0 else below,
        )

    def full_copy(kind, lo, count, side, part):
        cut = lo + part * (count // 2)
        cols = slice(cut, cut + count // 2)
        src = buf.up_out if side == 0 else buf.down_out
        dst = buf.full_minus if side == 0 else buf.full_plus
        return remote(
            src.at[:, cols],
            dst.at[:, cols],
            kind.full_send.at[2 * side + part],
            kind.full_recv.at[2 * side + part],
            above if side == 0 else below,
        )

    def pass_on(kind, lo, count, side, part):
        acc = buf.up_acc if side == 0 else buf.down_acc
        out = buf.up_out if side == 0 else buf.down_out
        got = buf.half_minus if side == 0 else buf.half_plus
        cut = lo + part * (count // 2)
        cols = slice(cut, cut + count // 2)
        value = acc[:, cols]
        if part == side:
            half_copy(kind, lo, count, side).wait_recv()
            value = value + got[:, cols].astype(F32)
        out[:, cols] = value.astype(BF16)
        full_copy(kind, lo, count, side, part).start()

    def multiply(big, kind, lo, count, t, ref):
        sib_step(big, kind, t)
        for q in range(lo, lo + count, 256):
            ref[:, q : q + 256] = dot(big[tokens(t), :], w[:, q : q + 256]).astype(ref.dtype)

    def multiply_step(big, kind, lo, count, r):
        if r == 0:
            multiply(big, kind, lo, count, d, buf.own_acc)
        elif r == 1:
            multiply(big, kind, lo, count, up, buf.up_acc)
            pass_on(kind, lo, count, 0, 1)
        elif r == 3:
            multiply(big, kind, lo, count, down, buf.down_acc)
            pass_on(kind, lo, count, 1, 0)
        else:
            multiply(big, kind, lo, count, across, buf.far_out)
            half_copy(kind, lo, count, 0).start()
            half_copy(kind, lo, count, 1).start()

    def finish_depth(kind, lo, count):
        cols = slice(lo, lo + count)
        for side in range(2):
            full_copy(kind, lo, count, side, 0).wait_recv()
            full_copy(kind, lo, count, side, 1).wait_recv()
        buf.own_acc[:, cols] = (
            buf.own_acc[:, cols]
            + buf.full_minus[:, cols].astype(F32)
            + buf.full_plus[:, cols].astype(F32)
        )

    def drain_depth(kind, lo, count):
        for side in range(2):
            half_copy(kind, lo, count, side).wait_send()
            full_copy(kind, lo, count, side, 0).wait_send()
            full_copy(kind, lo, count, side, 1).wait_send()

    def ring_block(ref, step, t):
        half = ref.shape[1] // 2
        second = step in (1, 2, 5)
        return ref.at[tokens(t), half:] if second else ref.at[tokens(t), :half]

    def ring_copy(ref, kind, step):
        block = ring_block(ref, step, (d, d, d, d, down, up)[step])
        return remote(
            block,
            block,
            kind.ring_send.at[step],
            kind.ring_recv.at[step],
            above if step % 2 == 0 else below,
        )

    def ring_wait(ref, kind, step):
        block = ring_block(ref, step, (down, up, down, up, across, across)[step])
        remote(
            block,
            block,
            kind.ring_send.at[step],
            kind.ring_recv.at[step],
            above if step % 2 == 0 else below,
        ).wait_recv()

    def ring_start(ref, kind):
        ring_copy(ref, kind, 0).start()
        ring_copy(ref, kind, 1).start()

    def ring_more(ref, kind):
        for step in range(2):
            ring_copy(ref, kind, step).wait_send()
            ring_copy(ref, kind, step + 2).start()

    def ring_forward(ref, kind):
        for step in range(2):
            ring_wait(ref, kind, step)
            ring_copy(ref, kind, step + 2).wait_send()
            ring_copy(ref, kind, step + 4).start()

    def ring_near(ref, kind):
        ring_wait(ref, kind, 2)
        ring_wait(ref, kind, 3)

    def ring_far(ref, kind):
        ring_wait(ref, kind, 4)
        ring_wait(ref, kind, 5)

    def r_sib(kind, t, i):
        slot = 2 * t + i
        return remote(
            kind.sib_out.at[slot],
            kind.sib_in.at[slot],
            kind.r_sib_send.at[slot],
            kind.r_sib_recv.at[slot],
            sibling,
        )

    def r_far(kind, t, side):
        slot = 2 * t + side
        return remote(
            kind.far_out.at[slot],
            kind.far_in.at[slot],
            kind.r_far_send.at[slot],
            kind.r_far_recv.at[slot],
            (right, left)[side],
        )

    def r_side(kind, t, side):
        slot = 2 * t + side
        return remote(
            kind.side_out.at[slot],
            kind.side_in.at[slot],
            kind.r_side_send.at[slot],
            kind.r_side_recv.at[slot],
            (right, left)[side],
        )

    def r_mate(kind, t):
        return remote(
            kind.next_out.at[t],
            kind.mate_in.at[t],
            kind.r_next_send.at[t],
            kind.r_mate_recv.at[t],
            mate,
        )

    def r_last(kind, t, act):
        slot = place // 2 if kind is branch else 2 * (place // 2) + z
        dst = kind.last_in.at[slot]
        recv = kind.r_last_recv.at[slot]
        src = kind.next_out.at[t]
        section = section_up if kind is branch else s
        copy = remote(src, dst, kind.r_next_send.at[t], recv, at(t, d // 2, owner_x, c, section))

        def away():
            if act == "start":
                copy.start()
            else:
                copy.wait_send()

        if kind is branch:
            away()
        else:
            here = jnp.logical_and(t == d, jnp.logical_and(place < 2, z == d // 2))
            pl.when(jnp.logical_not(here))(away)

            @pl.when(here)
            def _():
                if act == "start":
                    pltpu.make_async_copy(src, dst, recv).start()

    def total_of(kind, t, x_, lo, count):
        p = (x_ - base + 4) % 4
        slot = 2 * t + ((p + 1) // 2) % 2
        rows = pl.ds(pl.multiple_of((p // 2) * HALF + lo, QUARTER), count)
        return kind.keep[slot, rows, :] + kind.sib_in[slot, rows, :].astype(F32)

    def first_stage(ref, kind, lo, t):
        count = ref.shape[1]
        left = ref[tokens(t), :]
        for i in range(2):
            rows = features(2 * i + 1 - c)
            value = dot_nt(left, w[rows, lo : lo + count])
            kind.sib_out[2 * t + i] = value.astype(BF16)
            r_sib(kind, t, i).start()
        for i in range(2):
            rows = features(2 * i + c)
            kind.keep[2 * t + i] = dot_nt(left, w[rows, lo : lo + count])

    def second_stage(kind, t):
        r_sib(kind, t, 0).wait_recv()
        r_sib(kind, t, 1).wait_recv()
        for side in range(2):
            value = total_of(kind, t, places[3], side * QUARTER, QUARTER)
            kind.far_out[2 * t + side] = value.astype(BF16)
            r_far(kind, t, side).start()

    def third_stage(kind, t):
        for side in range(2):
            slot = 2 * t + side
            r_far(kind, t, side).wait_recv()
            for part in range(2):
                value = total_of(kind, t, places[2 - side], part * QUARTER, QUARTER)
                if part == side:
                    value = value + kind.far_in[slot].astype(F32)
                kind.side_out[slot, part * QUARTER : (part + 1) * QUARTER, :] = value.astype(BF16)
            r_side(kind, t, side).start()

    def side_done(kind, t):
        r_side(kind, t, 0).wait_send()
        r_side(kind, t, 1).wait_send()

    def fourth_stage(kind, t):
        r_side(kind, t, 0).wait_recv()
        r_side(kind, t, 1).wait_recv()
        total = total_of(kind, t, x, 0, HALF)
        total = total + kind.side_in[2 * t].astype(F32) + kind.side_in[2 * t + 1].astype(F32)
        if kind is inputs:
            kind.next_out[t] = total.astype(BF16)
            r_last(kind, t, "start")
            return
        kind.total[t] = total

        @pl.when(z != entry(t, d))
        def _():
            kind.next_out[t] = total.astype(BF16)
            r_mate(kind, t).start()

    def fifth_stage(kind, t):
        @pl.when(z == entry(t, d))
        def _():
            r_mate(kind, t).wait_recv()
            total = kind.total[t] + kind.mate_in[t].astype(F32)
            kind.next_out[t] = total.astype(BF16)
            r_last(kind, t, "start")

    def last_stage(kind):
        count = 2 if kind is branch else 4
        for slot in range(count):
            remote(
                kind.last_in.at[slot],
                kind.last_in.at[slot],
                kind.r_next_send.at[0],
                kind.r_last_recv.at[slot],
                sibling,
            ).wait_recv()
        if kind is branch:
            return kind.last_in[0:2].reshape(SEQ, FEATURES).astype(F32)
        halves = [
            kind.last_in[2 * h].astype(F32) + kind.last_in[2 * h + 1].astype(F32) for h in range(2)
        ]
        return jnp.concatenate(halves, axis=0)

    def drain_reduce(kind):
        for t in range(4):
            r_sib(kind, t, 0).wait_send()
            r_sib(kind, t, 1).wait_send()
            r_far(kind, t, 0).wait_send()
            r_far(kind, t, 1).wait_send()

            if kind is inputs:
                r_last(kind, t, "wait")
                continue

            @pl.when(z != entry(t, d))
            def _():
                r_mate(kind, t).wait_send()

            @pl.when(z == entry(t, d))
            def _():
                r_last(kind, t, "wait")

    def stat_copy(name, k):
        return remote(
            name.out,
            name.slots.at[g],
            name.send.at[k],
            name.recv.at[k],
            (s, d, (g + k) % GRID),
        )

    lane = lax.broadcasted_iota(jnp.int32, (SEQ, HEAD), 1)

    def stat_start(name, first, second):
        both = jnp.where(lane == 0, first, jnp.where(lane == 1, second, 0.0))
        turned = both.T[0:8]
        name.out[...] = turned
        name.slots[g] = turned
        for k in range(1, GRID):
            stat_copy(name, k).start()

    def stat_finish(name):
        slots = name.slots
        for k in range(1, GRID):
            slot = slots.at[(g + GRID - k) % GRID]
            remote(
                slot, slot, name.send.at[k], name.recv.at[k], sibling
            ).wait_recv()
        total = jnp.sum(slots[...], axis=0)
        padded = jnp.concatenate([total, jnp.zeros((HEAD - 8, SEQ), F32)], axis=0)
        columns = padded.T
        return columns[:, 0:1], columns[:, 1:2]

    def stat_drain(name):
        for k in range(1, GRID):
            stat_copy(name, k).wait_send()

    def small_copy(name, k):
        return remote(
            name.out,
            name.slots.at[d],
            name.send.at[k],
            name.recv.at[k],
            at((d + k) % 4, z, x, c),
        )

    def small_start(name):
        name.slots[d] = name.out[...]
        for k in range(1, 4):
            small_copy(name, k).start()

    def small_finish(name):
        slots = name.slots
        for k in range(1, 4):
            slot = slots.at[(d + 4 - k) % 4]
            remote(
                slot, slot, name.send.at[k], name.recv.at[k], above
            ).wait_recv()
        return jnp.sum(slots[...], axis=0)

    def small_drain(name):
        for k in range(1, 4):
            small_copy(name, k).wait_send()

    xs = (buf.big_x, acts)
    cs = (buf.big_c, cots)
    xw = (0, QKV)
    cw = (QKV, 256)
    def weight_qkv(k):
        rows = slice(k * 256, (k + 1) * 256)
        dw_ref[rows, 0:QKV] = dot_tn(buf.big_x[:, rows], buf.dp[...]).astype(BF16)

    def weight_out(k):
        rows = slice(k * 256, (k + 1) * 256)
        dw_ref[rows, QKV:COLS] = dot_tn(buf.big_c[:, rows], buf.att[...]).astype(BF16)

    def relayout(k, _):
        rows = pl.ds(pl.multiple_of(k * 128, 128), 128)
        chunk = buf.raw[rows]
        for part in range(4):
            w[rows, part * 256 : (part + 1) * 256] = chunk[:, part, :]
        return 0

    def relayout_all():
        w_copy.wait()
        lax.fori_loop(0, ROWS // 128, relayout, 0)

    own_send(cot_ref.at[0], buf.big_c, cots)
    values = x_ref[0].astype(F32)
    stat_start(
        stat_a,
        jnp.sum(values, axis=-1, keepdims=True),
        jnp.sum(values * values, axis=-1, keepdims=True),
    )
    relayout_all()
    first, second = stat_finish(stat_a)
    width = 4 * ROWS
    centre = first / width
    reciprocal = lax.rsqrt(second / width - centre * centre + EPSILON)
    gain = ng_ref[...].astype(F32)
    centred = (x_ref[0].astype(F32) - centre) * reciprocal
    buf.centred[...] = centred
    buf.recip[...] = jnp.broadcast_to(reciprocal, (SEQ, HEAD))
    buf.norm[...] = (centred * gain).astype(BF16)
    near_step(*cs, down)
    near_step(*cs, across)
    own_send(buf.norm, buf.big_x, acts)
    near_step(*cs, up)
    side_step(*cs, down)
    side_step(*cs, across)
    near_step(*cs, d)
    side_step(*cs, up)
    far_step(*cs, across)
    near_step(*xs, across)
    multiply_step(*cs, *cw, 2)
    near_step(*xs, up)
    side_step(*xs, across)
    far_step(*cs, up)
    near_step(*xs, down)
    far_step(*cs, down)
    near_step(*xs, d)
    far_step(*xs, across)
    multiply_step(*cs, *cw, 3)
    multiply_step(*xs, *xw, 2)
    side_step(*xs, down)
    side_step(*cs, d)
    side_sent(*xs, up)
    multiply_step(*cs, *cw, 1)
    side_step(*xs, d)
    side_step(*xs, up)
    far_step(*cs, d)
    far_step(*xs, up)
    far_step(*xs, down)
    multiply_step(*xs, *xw, 3)
    side_sent(*cs, down)
    pass_on(cots, *cw, 0, 0)
    multiply_step(*xs, *xw, 1)
    multiply_step(*cs, *cw, 0)
    far_step(*xs, d)
    pass_on(acts, *xw, 1, 1)
    pass_on(cots, *cw, 1, 1)
    multiply_step(*xs, *xw, 0)
    pass_on(acts, *xw, 0, 0)
    finish_depth(acts, *xw)
    own = buf.own_acc
    for h in range(2):
        cols = [slice(part * 256 + h * HEAD, part * 256 + (h + 1) * HEAD) for part in range(4)]
        for part in range(2):
            hat, rec = normalize(own[:, cols[part]])
            buf.hats[2 * part + h] = hat
            buf.recs[2 * part + h] = jnp.broadcast_to(rec, (SEQ, HEAD))
            row = hg_ref[0, part, h : h + 1, :].astype(F32)
            buf.lows[2 * part + h] = (hat * row).astype(BF16)
        buf.lows[4 + h] = own[:, cols[2]].astype(BF16)
        scores = dot_nt(buf.lows[h], buf.lows[2 + h]) * SCALE
        exponent = jnp.exp(scores)
        attention = exponent / jnp.sum(exponent, axis=-1, keepdims=True)
        buf.attention[h] = attention
        attended = dot(attention.astype(BF16), buf.lows[4 + h])
        buf.att[tokens(d), h * HEAD : (h + 1) * HEAD] = attended.astype(BF16)
    ring_start(buf.att, cots)
    ring_more(buf.att, cots)
    finish_depth(cots, *cw)
    gains.out[...] = jnp.zeros((8, HEAD), F32)
    for h in range(2):
        d_attended = own[:, QKV + h * HEAD : QKV + (h + 1) * HEAD].astype(BF16)
        attention = buf.attention[h]
        d_attention = dot_nt(d_attended, buf.lows[4 + h])
        row_delta = jnp.sum(attention * d_attention, axis=-1, keepdims=True)
        d_score = (attention * (d_attention - row_delta) * SCALE).astype(BF16)
        d_query = dot(d_score, buf.lows[2 + h])
        d_key = dot_tn(d_score, buf.lows[h])
        d_value = dot_tn(attention.astype(BF16), d_attended)
        for part, upstream in enumerate((d_query, d_key)):
            hat = buf.hats[2 * part + h]
            row = hg_ref[0, part, h : h + 1, :].astype(F32)
            grad = normalize_back(upstream, hat, buf.recs[2 * part + h][:, 0:1], row)
            at_col = part * 256 + h * HEAD
            buf.dp[tokens(d), at_col : at_col + HEAD] = grad.astype(BF16)
            index = 2 * part + h
            gains.out[index : index + 1, :] = jnp.sum(upstream * hat, axis=0, keepdims=True)
        at_col = 512 + h * HEAD
        buf.dp[tokens(d), at_col : at_col + HEAD] = d_value.astype(BF16)
    small_start(gains)
    first_stage(buf.att, branch, QKV, d)
    ring_start(buf.dp, acts)
    second_stage(branch, d)
    ring_forward(buf.att, cots)
    first_stage(buf.dp, inputs, 0, d)
    ring_near(buf.att, cots)
    first_stage(buf.att, branch, QKV, down)
    first_stage(buf.att, branch, QKV, up)
    second_stage(branch, down)
    ring_more(buf.dp, acts)
    second_stage(branch, up)
    third_stage(branch, down)
    third_stage(branch, up)
    ring_far(buf.att, cots)
    side_sent(*xs, across)
    second_stage(inputs, d)
    third_stage(branch, d)
    first_stage(buf.att, branch, QKV, across)
    fourth_stage(branch, down)
    side_sent(*xs, down)
    side_done(branch, up)
    ring_forward(buf.dp, acts)
    ring_near(buf.dp, acts)
    second_stage(branch, across)
    side_done(branch, d)
    fourth_stage(branch, up)
    first_stage(buf.dp, inputs, 0, up)
    third_stage(inputs, d)
    weight_out(5)
    third_stage(branch, across)
    second_stage(inputs, up)
    first_stage(buf.dp, inputs, 0, down)
    fifth_stage(branch, up)
    fifth_stage(branch, down)
    side_sent(*cs, up)
    second_stage(inputs, down)
    fourth_stage(branch, d)
    weight_out(1)
    third_stage(inputs, up)
    third_stage(inputs, down)
    weight_out(4)
    ring_far(buf.dp, acts)
    first_stage(buf.dp, inputs, 0, across)
    second_stage(inputs, across)
    side_sent(*xs, d)
    side_done(inputs, down)
    fourth_stage(branch, across)
    fifth_stage(branch, d)
    weight_qkv(2)
    fourth_stage(inputs, down)
    side_done(inputs, up)
    weight_qkv(1)
    side_sent(*cs, across)
    third_stage(inputs, across)
    weight_qkv(0)
    weight_out(0)
    weight_out(3)
    side_done(inputs, d)
    fourth_stage(inputs, up)
    weight_qkv(5)
    side_sent(*cs, d)
    weight_qkv(3)
    side_done(inputs, across)
    side_done(branch, down)
    fourth_stage(inputs, d)
    fourth_stage(inputs, across)
    weight_qkv(4)
    d_normed = last_stage(inputs)
    weighted = d_normed * gain
    centred = buf.centred[...]
    stat_start(
        stat_b,
        jnp.sum(weighted, axis=-1, keepdims=True),
        jnp.sum(weighted * centred, axis=-1, keepdims=True),
    )
    norms.out[...] = jnp.broadcast_to(
        jnp.sum(d_normed * centred, axis=0, keepdims=True), (8, FEATURES)
    )
    small_start(norms)
    total = small_finish(gains)
    for part in range(2):
        hgg_ref[0, part] = total[2 * part : 2 * part + 2]
    first, second = stat_finish(stat_b)
    reciprocal = buf.recip[:, 0:1]
    grad = reciprocal * (weighted - first / width - centred * (second / width))
    buf.grad_out[...] = grad.astype(BF16)
    grad_copy = remote(
        buf.grad_out,
        buf.grad_in,
        sems.grad_send.at[0],
        sems.grad_recv.at[0],
        (section_down, d, g),
    )
    grad_copy.start()
    ngg_ref[...] = small_finish(norms)[0:1]
    drain_gather(cot_ref.at[0], buf.big_c, cots)
    drain_gather(buf.norm, buf.big_x, acts)
    drain_depth(acts, 0, QKV)
    drain_depth(cots, QKV, 256)
    for step in range(4, 6):
        ring_copy(buf.att, cots, step).wait_send()
        ring_copy(buf.dp, acts, step).wait_send()
    fifth_stage(branch, across)
    side_done(branch, across)
    weight_out(2)
    nb_ref[0] = last_stage(branch).astype(BF16)
    drain_reduce(branch)
    drain_reduce(inputs)
    stat_drain(stat_a)
    stat_drain(stat_b)
    small_drain(gains)
    small_drain(norms)
    grad_copy.wait()
    rg_ref[0] = buf.grad_in[...]


def local(section_input, cotangent, projections, norm_gain, head_gains):
    here = pl.BlockSpec(memory_space=pltpu.VMEM)
    outs = pl.pallas_call(
        kernel,
        out_shape=(
            jax.ShapeDtypeStruct((1, SEQ, FEATURES), BF16),
            jax.ShapeDtypeStruct((1, SEQ, FEATURES), BF16),
            jax.ShapeDtypeStruct((ROWS, COLS), BF16),
            jax.ShapeDtypeStruct((1, FEATURES), F32),
            jax.ShapeDtypeStruct((1, 2, 2, HEAD), F32),
        ),
        in_specs=[here, here, pl.BlockSpec(memory_space=pl.ANY), here, here],
        out_specs=(here,) * 5,
        scratch_shapes=LEAVES,
        compiler_params=pltpu.CompilerParams(
            collective_id=0, has_side_effects=True, vmem_limit_bytes=60 * 1024 * 1024
        ),
        name="block",
    )(section_input, cotangent, projections, norm_gain, head_gains)
    next_branch, returned, weight_grad, norm_total, head_total = outs
    return (
        next_branch,
        returned,
        weight_grad.reshape(1, ROWS, 4, 256),
        norm_total,
        head_total,
    )


def solution(mesh):
    in_specs = (
        P("section", "depth", "grid"),
        P("section", "depth", "grid"),
        P("section", "depth", None, "grid"),
        P("section", "grid"),
        P("section", None, "grid", None),
    )
    out_specs = (
        P("section", "depth", "grid"),
        P("section", "depth", "grid"),
        P("section", "depth", None, "grid"),
        P("section", "grid"),
        P("section", None, "grid", None),
    )
    return jax.shard_map(local, mesh=mesh, in_specs=in_specs, out_specs=out_specs, check_vma=False)
```

```python
from types import SimpleNamespace

import jax
import jax.numpy as jnp
from jax import lax
from jax.experimental import pallas as pl
from jax.experimental.pallas import tpu as pltpu
from jax.sharding import PartitionSpec as P

SEQ = 256
HALF = 128
QUARTER = 64
EPSILON = 1e-06
MESH = pl.DeviceIdType.MESH
BF16 = jnp.bfloat16
F32 = jnp.float32
FEATURES = 384
ROWS = 1536
HEAD = 128
QKV = 768
COLS = 1024
GRID = 16
SCALE = HEAD ** (-0.5)


def remote(src, dst, send_sem, recv_sem, device):
    return pltpu.make_async_remote_copy(
        src_ref=src,
        dst_ref=dst,
        send_sem=send_sem,
        recv_sem=recv_sem,
        device_id=device,
        device_id_type=MESH,
    )


def normalize(values):
    centre = jnp.mean(values, axis=-1, keepdims=True)
    second = jnp.mean(values * values, axis=-1, keepdims=True)
    reciprocal = lax.rsqrt(second - centre * centre + EPSILON)
    return (values - centre) * reciprocal, reciprocal


def normalize_back(upstream, normed, reciprocal, gain_row):
    scaled = upstream * gain_row
    first_mean = jnp.mean(scaled, axis=-1, keepdims=True)
    second_mean = jnp.mean(scaled * normed, axis=-1, keepdims=True)
    return reciprocal * (scaled - first_mean - normed * second_mean)


def dot(a, b):
    return jnp.dot(a, b, preferred_element_type=F32)


def dot_nt(a, b):
    return lax.dot_general(a, b, (((1,), (1,)), ((), ())), preferred_element_type=F32)


def dot_tn(a, b):
    return lax.dot_general(a, b, (((0,), (0,)), ((), ())), preferred_element_type=F32)


def vmem(shape, dtype):
    return pltpu.VMEM(shape, dtype)


def dma(count):
    return pltpu.SemaphoreType.DMA((count,))


def gather_scratch():
    return dict(
        own_send=dma(4),
        near_recv=dma(4),
        side_send=dma(8),
        side_recv=dma(8),
        far_send=dma(8),
        far_recv=dma(8),
        sib_send=dma(16),
        sib_recv=dma(16),
        half_send=dma(2),
        half_recv=dma(2),
        full_send=dma(4),
        full_recv=dma(4),
        ring_send=dma(6),
        ring_recv=dma(6),
    )


def reduce_scratch():
    return dict(
        sib_out=vmem((8, SEQ, FEATURES), BF16),
        sib_in=vmem((8, SEQ, FEATURES), BF16),
        keep=vmem((8, SEQ, FEATURES), F32),
        far_out=vmem((8, QUARTER, FEATURES), BF16),
        far_in=vmem((8, QUARTER, FEATURES), BF16),
        side_out=vmem((8, HALF, FEATURES), BF16),
        side_in=vmem((8, HALF, FEATURES), BF16),
        total=vmem((4, HALF, FEATURES), F32),
        next_out=vmem((4, HALF, FEATURES), BF16),
        mate_in=vmem((4, HALF, FEATURES), BF16),
        last_in=vmem((4, HALF, FEATURES), BF16),
        r_sib_send=dma(8),
        r_sib_recv=dma(8),
        r_far_send=dma(8),
        r_far_recv=dma(8),
        r_side_send=dma(8),
        r_side_recv=dma(8),
        r_next_send=dma(4),
        r_mate_recv=dma(4),
        r_last_recv=dma(4),
    )


def sum_scratch(count, rows, columns):
    return dict(
        out=vmem((rows, columns), F32),
        slots=vmem((count, rows, columns), F32),
        send=dma(count),
        recv=dma(count),
    )


SCRATCH = dict(
    acts=gather_scratch(),
    cots=gather_scratch(),
    branch=reduce_scratch(),
    inputs=reduce_scratch(),
    stat_a=sum_scratch(GRID, 8, SEQ + FEATURES),
    sums=sum_scratch(4, 8, QKV),
    stat_b=sum_scratch(GRID, 8, SEQ),
    gains=sum_scratch(4, 8, HEAD),
    norms=sum_scratch(4, 8, FEATURES),
    sems=dict(w=dma(1), grad_send=dma(1), grad_recv=dma(1)),
    buf=dict(
        w=vmem((ROWS, COLS), BF16),
        raw=vmem((ROWS, 4, 256), BF16),
        norm=vmem((SEQ, FEATURES), BF16),
        centred=vmem((SEQ, FEATURES), F32),
        recip=vmem((SEQ, HEAD), F32),
        big_x=vmem((4 * SEQ, ROWS), BF16),
        big_c=vmem((4 * SEQ, ROWS), BF16),
        far_out=vmem((SEQ, COLS), BF16),
        up_out=vmem((SEQ, COLS), BF16),
        down_out=vmem((SEQ, COLS), BF16),
        half_minus=vmem((SEQ, COLS), BF16),
        half_plus=vmem((SEQ, COLS), BF16),
        full_minus=vmem((SEQ, COLS), BF16),
        full_plus=vmem((SEQ, COLS), BF16),
        up_acc=vmem((SEQ, COLS), F32),
        down_acc=vmem((SEQ, COLS), F32),
        own_acc=vmem((SEQ, COLS), F32),
        attention=vmem((2, SEQ, SEQ), F32),
        hats=vmem((4, SEQ, HEAD), F32),
        recs=vmem((4, SEQ, HEAD), F32),
        lows=vmem((6, SEQ, HEAD), BF16),
        att=vmem((4 * SEQ, 256), BF16),
        dp=vmem((4 * SEQ, QKV), BF16),
        grad_out=vmem((SEQ, FEATURES), BF16),
        grad_in=vmem((SEQ, FEATURES), BF16),
    ),
)
LEAVES, TREE = jax.tree.flatten(SCRATCH)


def kernel(*refs):
    x_ref, cot_ref, w_hbm, ng_ref, hg_ref = refs[:5]
    nb_ref, rg_ref, dw_ref, ngg_ref, hgg_ref = refs[5:10]
    parts = jax.tree.unflatten(TREE, refs[10:])
    parts = {name: SimpleNamespace(**part) for name, part in parts.items()}
    acts, cots, branch, inputs = (parts[name] for name in ("acts", "cots", "branch", "inputs"))
    stat_a, stat_b = parts["stat_a"], parts["stat_b"]
    gains, norms, sums = parts["gains"], parts["norms"], parts["sums"]
    sems, buf = parts["sems"], parts["buf"]
    w = buf.w

    s = lax.axis_index("section")
    d = lax.axis_index("depth")
    g = lax.axis_index("grid")
    z = g // 8
    x = (g // 2) % 4
    c = g % 2
    base = 2 * (d % 2)
    place = (x - base + 4) % 4
    up = (d + 1) % 4
    down = (d + 3) % 4
    across = (d + 2) % 4

    def at(depth, z_, x_, c_, section=None):
        return (s if section is None else section, depth, z_ * 8 + x_ * 2 + c_)

    sibling = at(d, z, x, 1 - c)
    left_x = (x + 3) % 4
    right_x = (x + 1) % 4
    places = (x, left_x, right_x, (x + 2) % 4)
    left = at(d, z, left_x, c)
    right = at(d, z, right_x, c)
    above = at(up, z, x, c)
    below = at(down, z, x, c)
    section_up = (s + 1) % 4
    section_down = (s + 3) % 4
    home = g // 4
    home_block = g % 4
    home_base = 2 * (home % 2)
    home_other = (home_base + 3 - (x - home_base + 4) % 4) % 4
    owner_x = base + ((place + 1) // 2) % 2
    mate = at(d, 1 - z, x, c)

    def entry(t, depth):
        k = (t - depth + 4) % 4
        middle = depth // 2
        return (k % 2) * ((3 - k) // 2) + (1 - k % 2) * (middle + (k // 2) * (1 - 2 * middle))


    barrier = pltpu.get_barrier_semaphore()

    def greet(device):
        pl.semaphore_signal(barrier, inc=1, device_id=device, device_id_type=MESH)

    for k in range(1, GRID):
        greet((s, d, (g + k) % GRID))
    for k in range(1, 4):
        greet(at((d + k) % 4, z, x, c))
        greet(at((d + k) % 4, d // 2, owner_x, c))
    greet((section_up, d, g))
    for zz in range(2):
        for xx in (x, home_other):
            greet(at(home, zz, xx, c, section_down))

    @pl.when(home != d)
    def _():
        for zz in range(2):
            for xx in (x, home_other):
                greet(at(home, zz, xx, c))

    pl.semaphore_wait(barrier, 26 + 4 * (((home - d + 4) % 4 + 3) // 4))

    w_copy = pltpu.make_async_copy(w_hbm.at[0], buf.raw, sems.w.at[0])
    w_copy.start()

    def tokens(t):
        return pl.ds(pl.multiple_of(t * SEQ, SEQ), SEQ)

    def features(j):
        return pl.ds(pl.multiple_of(j * FEATURES, FEATURES), FEATURES)

    def own_copy(src, big, kind, h, zz):
        rows = pl.ds(pl.multiple_of(d * SEQ + h * HALF, HALF), HALF)
        return remote(
            src.at[h * HALF : (h + 1) * HALF, :],
            big.at[rows, features(home_block)],
            kind.own_send.at[2 * h + zz],
            kind.near_recv.at[d],
            at(home, zz, home_other if h else x, c),
        )

    def own_send(src, big, kind):
        for zz in range(2):
            here = jnp.logical_and(home == d, z == zz)

            @pl.when(here)
            def _():
                pltpu.make_async_copy(
                    src.at[0:HALF, :],
                    big.at[pl.ds(pl.multiple_of(d * SEQ, SEQ), HALF), features(home_block)],
                    kind.near_recv.at[d],
                ).start()

            @pl.when(jnp.logical_not(here))
            def _():
                own_copy(src, big, kind, 0, zz).start()

            own_copy(src, big, kind, 1, zz).start()

    def block(big, t, x_, c_, lo=0, count=HALF):
        p = (x_ - base + 4) % 4
        start = pl.multiple_of(t * SEQ + (p // 2) * HALF + lo, QUARTER)
        return big.at[pl.ds(start, count), features(2 * (((p + 1) // 2) % 2) + c_)]

    def side_copy(big, kind, t, side, arriving=False):
        ref = block(big, t, places[1 + side] if arriving else x, c)
        slot = 2 * t + side
        return remote(
            ref, ref, kind.side_send.at[slot], kind.side_recv.at[slot], (right, left)[side]
        )

    def far_copy(big, kind, t, side, arriving=False):
        ref = block(big, t, places[3 if arriving else 1 + side], c, side * QUARTER, QUARTER)
        slot = 2 * t + side
        return remote(
            ref, ref, kind.far_send.at[slot], kind.far_recv.at[slot], (right, left)[side]
        )

    def sib_copy(big, kind, t, part, arriving=False):
        ref = block(big, t, places[part], 1 - c if arriving else c)
        slot = 4 * t + part
        return remote(ref, ref, kind.sib_send.at[slot], kind.sib_recv.at[slot], sibling)

    def near_step(big, kind, t):
        ref = block(big, t, x, c)
        remote(ref, ref, kind.side_send.at[2 * t], kind.near_recv.at[t], right).wait_recv()
        side_copy(big, kind, t, 0).start()
        side_copy(big, kind, t, 1).start()
        sib_copy(big, kind, t, 0).start()

    def side_sent(big, kind, t):
        side_copy(big, kind, t, 0).wait_send()
        side_copy(big, kind, t, 1).wait_send()

    def side_step(big, kind, t):
        for side in range(2):
            side_copy(big, kind, t, side, True).wait_recv()
            far_copy(big, kind, t, side).start()
            sib_copy(big, kind, t, 1 + side).start()

    def far_step(big, kind, t):
        far_copy(big, kind, t, 0, True).wait_recv()
        far_copy(big, kind, t, 1, True).wait_recv()
        sib_copy(big, kind, t, 3).start()

    def sib_step(big, kind, t):
        for part in range(4):
            sib_copy(big, kind, t, part, True).wait_recv()

    def drain_gather(src, big, kind):
        for zz in range(2):

            @pl.when(jnp.logical_or(home != d, z != zz))
            def _():
                own_copy(src, big, kind, 0, zz).wait_send()

            own_copy(src, big, kind, 1, zz).wait_send()
        for t in range(4):
            for part in range(4):
                sib_copy(big, kind, t, part).wait_send()
            far_copy(big, kind, t, 0).wait_send()
            far_copy(big, kind, t, 1).wait_send()

    def half_copy(kind, lo, count, side):
        cut = lo + side * (count // 2)
        cols = slice(cut, cut + count // 2)
        dst = buf.half_minus if side == 0 else buf.half_plus
        return remote(
            buf.far_out.at[:, cols],
            dst.at[:, cols],
            kind.half_send.at[side],
            kind.half_recv.at[side],
            above if side == 0 else below,
        )

    def full_copy(kind, lo, count, side, part):
        cut = lo + part * (count // 2)
        cols = slice(cut, cut + count // 2)
        src = buf.up_out if side == 0 else buf.down_out
        dst = buf.full_minus if side == 0 else buf.full_plus
        return remote(
            src.at[:, cols],
            dst.at[:, cols],
            kind.full_send.at[2 * side + part],
            kind.full_recv.at[2 * side + part],
            above if side == 0 else below,
        )

    def pass_on(kind, lo, count, side, part):
        acc = buf.up_acc if side == 0 else buf.down_acc
        out = buf.up_out if side == 0 else buf.down_out
        got = buf.half_minus if side == 0 else buf.half_plus
        cut = lo + part * (count // 2)
        cols = slice(cut, cut + count // 2)
        value = acc[:, cols]
        if part == side:
            half_copy(kind, lo, count, side).wait_recv()
            value = value + got[:, cols].astype(F32)
        out[:, cols] = value.astype(BF16)
        full_copy(kind, lo, count, side, part).start()

    def multiply(big, kind, lo, count, t, ref):
        sib_step(big, kind, t)
        for q in range(lo, lo + count, 256):
            ref[:, q : q + 256] = dot(big[tokens(t), :], w[:, q : q + 256]).astype(ref.dtype)

    def multiply_step(big, kind, lo, count, r):
        if r == 0:
            multiply(big, kind, lo, count, d, buf.own_acc)
        elif r == 1:
            multiply(big, kind, lo, count, up, buf.up_acc)
            pass_on(kind, lo, count, 0, 1)
        elif r == 3:
            multiply(big, kind, lo, count, down, buf.down_acc)
            pass_on(kind, lo, count, 1, 0)
        else:
            multiply(big, kind, lo, count, across, buf.far_out)
            half_copy(kind, lo, count, 0).start()
            half_copy(kind, lo, count, 1).start()

    def finish_depth(kind, lo, count):
        cols = slice(lo, lo + count)
        for side in range(2):
            full_copy(kind, lo, count, side, 0).wait_recv()
            full_copy(kind, lo, count, side, 1).wait_recv()
        buf.own_acc[:, cols] = (
            buf.own_acc[:, cols]
            + buf.full_minus[:, cols].astype(F32)
            + buf.full_plus[:, cols].astype(F32)
        )

    def drain_depth(kind, lo, count):
        for side in range(2):
            half_copy(kind, lo, count, side).wait_send()
            full_copy(kind, lo, count, side, 0).wait_send()
            full_copy(kind, lo, count, side, 1).wait_send()

    def ring_block(ref, step, t):
        half = ref.shape[1] // 2
        second = step in (1, 2, 5)
        return ref.at[tokens(t), half:] if second else ref.at[tokens(t), :half]

    def ring_copy(ref, kind, step):
        block = ring_block(ref, step, (d, d, d, d, down, up)[step])
        return remote(
            block,
            block,
            kind.ring_send.at[step],
            kind.ring_recv.at[step],
            above if step % 2 == 0 else below,
        )

    def ring_wait(ref, kind, step):
        block = ring_block(ref, step, (down, up, down, up, across, across)[step])
        remote(
            block,
            block,
            kind.ring_send.at[step],
            kind.ring_recv.at[step],
            above if step % 2 == 0 else below,
        ).wait_recv()

    def ring_start(ref, kind):
        ring_copy(ref, kind, 0).start()
        ring_copy(ref, kind, 1).start()

    def ring_more(ref, kind):
        for step in range(2):
            ring_copy(ref, kind, step).wait_send()
            ring_copy(ref, kind, step + 2).start()

    def ring_forward(ref, kind):
        for step in range(2):
            ring_wait(ref, kind, step)
            ring_copy(ref, kind, step + 2).wait_send()
            ring_copy(ref, kind, step + 4).start()

    def ring_near(ref, kind):
        ring_wait(ref, kind, 2)
        ring_wait(ref, kind, 3)

    def ring_far(ref, kind):
        ring_wait(ref, kind, 4)
        ring_wait(ref, kind, 5)

    def r_sib(kind, t, i):
        slot = 2 * t + i
        return remote(
            kind.sib_out.at[slot],
            kind.sib_in.at[slot],
            kind.r_sib_send.at[slot],
            kind.r_sib_recv.at[slot],
            sibling,
        )

    def r_far(kind, t, side):
        slot = 2 * t + side
        return remote(
            kind.far_out.at[slot],
            kind.far_in.at[slot],
            kind.r_far_send.at[slot],
            kind.r_far_recv.at[slot],
            (right, left)[side],
        )

    def r_side(kind, t, side):
        slot = 2 * t + side
        return remote(
            kind.side_out.at[slot],
            kind.side_in.at[slot],
            kind.r_side_send.at[slot],
            kind.r_side_recv.at[slot],
            (right, left)[side],
        )

    def r_mate(kind, t):
        return remote(
            kind.next_out.at[t],
            kind.mate_in.at[t],
            kind.r_next_send.at[t],
            kind.r_mate_recv.at[t],
            mate,
        )

    def r_last(kind, t, act):
        slot = place // 2 if kind is branch else 2 * (place // 2) + z
        dst = kind.last_in.at[slot]
        recv = kind.r_last_recv.at[slot]
        src = kind.next_out.at[t]
        section = section_up if kind is branch else s
        copy = remote(src, dst, kind.r_next_send.at[t], recv, at(t, d // 2, owner_x, c, section))

        def away():
            if act == "start":
                copy.start()
            else:
                copy.wait_send()

        if kind is branch:
            away()
        else:
            here = jnp.logical_and(t == d, jnp.logical_and(place < 2, z == d // 2))
            pl.when(jnp.logical_not(here))(away)

            @pl.when(here)
            def _():
                if act == "start":
                    pltpu.make_async_copy(src, dst, recv).start()

    def total_of(kind, t, x_, lo, count):
        p = (x_ - base + 4) % 4
        slot = 2 * t + ((p + 1) // 2) % 2
        rows = pl.ds(pl.multiple_of((p // 2) * HALF + lo, QUARTER), count)
        return kind.keep[slot, rows, :] + kind.sib_in[slot, rows, :].astype(F32)

    def first_stage(ref, kind, lo, t):
        count = ref.shape[1]
        left = ref[tokens(t), :]
        for i in range(2):
            rows = features(2 * i + 1 - c)
            value = dot_nt(left, w[rows, lo : lo + count])
            kind.sib_out[2 * t + i] = value.astype(BF16)
            r_sib(kind, t, i).start()
        for i in range(2):
            rows = features(2 * i + c)
            kind.keep[2 * t + i] = dot_nt(left, w[rows, lo : lo + count])

    def second_stage(kind, t):
        r_sib(kind, t, 0).wait_recv()
        r_sib(kind, t, 1).wait_recv()
        for side in range(2):
            value = total_of(kind, t, places[3], side * QUARTER, QUARTER)
            kind.far_out[2 * t + side] = value.astype(BF16)
            r_far(kind, t, side).start()

    def third_stage(kind, t):
        for side in range(2):
            slot = 2 * t + side
            r_far(kind, t, side).wait_recv()
            for part in range(2):
                value = total_of(kind, t, places[2 - side], part * QUARTER, QUARTER)
                if part == side:
                    value = value + kind.far_in[slot].astype(F32)
                kind.side_out[slot, part * QUARTER : (part + 1) * QUARTER, :] = value.astype(BF16)
            r_side(kind, t, side).start()

    def side_done(kind, t):
        r_side(kind, t, 0).wait_send()
        r_side(kind, t, 1).wait_send()

    def fourth_stage(kind, t):
        r_side(kind, t, 0).wait_recv()
        r_side(kind, t, 1).wait_recv()
        total = total_of(kind, t, x, 0, HALF)
        total = total + kind.side_in[2 * t].astype(F32) + kind.side_in[2 * t + 1].astype(F32)
        if kind is inputs:
            kind.next_out[t] = total.astype(BF16)
            r_last(kind, t, "start")
            return
        kind.total[t] = total

        @pl.when(z != entry(t, d))
        def _():
            kind.next_out[t] = total.astype(BF16)
            r_mate(kind, t).start()

    def fifth_stage(kind, t):
        @pl.when(z == entry(t, d))
        def _():
            r_mate(kind, t).wait_recv()
            total = kind.total[t] + kind.mate_in[t].astype(F32)
            kind.next_out[t] = total.astype(BF16)
            r_last(kind, t, "start")

    def last_stage(kind):
        count = 2 if kind is branch else 4
        for slot in range(count):
            remote(
                kind.last_in.at[slot],
                kind.last_in.at[slot],
                kind.r_next_send.at[0],
                kind.r_last_recv.at[slot],
                sibling,
            ).wait_recv()
        if kind is branch:
            return kind.last_in[0:2].reshape(SEQ, FEATURES).astype(F32)
        halves = [
            kind.last_in[2 * h].astype(F32) + kind.last_in[2 * h + 1].astype(F32) for h in range(2)
        ]
        return jnp.concatenate(halves, axis=0)

    def drain_reduce(kind):
        for t in range(4):
            r_sib(kind, t, 0).wait_send()
            r_sib(kind, t, 1).wait_send()
            r_far(kind, t, 0).wait_send()
            r_far(kind, t, 1).wait_send()

            if kind is inputs:
                r_last(kind, t, "wait")
                continue

            @pl.when(z != entry(t, d))
            def _():
                r_mate(kind, t).wait_send()

            @pl.when(z == entry(t, d))
            def _():
                r_last(kind, t, "wait")

    def stat_copy(name, k):
        return remote(
            name.out,
            name.slots.at[g],
            name.send.at[k],
            name.recv.at[k],
            (s, d, (g + k) % GRID),
        )

    lane = lax.broadcasted_iota(jnp.int32, (SEQ, HEAD), 1)

    def stat_start(name, first, second):
        both = jnp.where(lane == 0, first, jnp.where(lane == 1, second, 0.0))
        turned = both.T[0:8]
        name.out[:, 0:SEQ] = turned
        if name is stat_a:
            name.out[:, SEQ:] = jnp.broadcast_to(ng_ref[...].astype(F32), (8, FEATURES))
        name.slots[g] = name.out[...]
        for k in range(1, GRID):
            stat_copy(name, k).start()

    def stat_finish(name):
        slots = name.slots
        for k in range(1, GRID):
            slot = slots.at[(g + GRID - k) % GRID]
            remote(
                slot, slot, name.send.at[k], name.recv.at[k], sibling
            ).wait_recv()
        total = jnp.sum(slots[:, :, 0:SEQ], axis=0)
        padded = jnp.concatenate([total, jnp.zeros((HEAD - 8, SEQ), F32)], axis=0)
        columns = padded.T
        return columns[:, 0:1], columns[:, 1:2]

    def stat_drain(name):
        for k in range(1, GRID):
            stat_copy(name, k).wait_send()

    def small_copy(name, k):
        return remote(
            name.out,
            name.slots.at[d],
            name.send.at[k],
            name.recv.at[k],
            at((d + k) % 4, z, x, c),
        )

    def small_start(name):
        name.slots[d] = name.out[...]
        for k in range(1, 4):
            small_copy(name, k).start()

    def small_finish(name):
        slots = name.slots
        for k in range(1, 4):
            slot = slots.at[(d + 4 - k) % 4]
            remote(
                slot, slot, name.send.at[k], name.recv.at[k], above
            ).wait_recv()
        return jnp.sum(slots[...], axis=0)

    def small_drain(name):
        for k in range(1, 4):
            small_copy(name, k).wait_send()

    xs = (buf.big_x, acts)
    cs = (buf.big_c, cots)
    xw = (0, QKV)
    cw = (QKV, 256)
    def weight_qkv(k):
        rows = slice(k * 256, (k + 1) * 256)
        dw_ref[rows, 0:QKV] = dot_tn(buf.big_x[:, rows], buf.dp[...]).astype(BF16)

    def weight_out(k):
        rows = slice(k * 256, (k + 1) * 256)
        dw_ref[rows, QKV:COLS] = dot_tn(buf.big_c[:, rows], buf.att[...]).astype(BF16)

    def relayout(k, _):
        rows = pl.ds(pl.multiple_of(k * 128, 128), 128)
        chunk = buf.raw[rows]
        for part in range(4):
            w[rows, part * 256 : (part + 1) * 256] = chunk[:, part, :]
        return 0

    def relayout_all():
        w_copy.wait()
        lax.fori_loop(0, ROWS // 128, relayout, 0)

    own_send(cot_ref.at[0], buf.big_c, cots)
    values = x_ref[0].astype(F32)
    stat_start(
        stat_a,
        jnp.sum(values, axis=-1, keepdims=True),
        jnp.sum(values * values, axis=-1, keepdims=True),
    )
    relayout_all()
    first, second = stat_finish(stat_a)
    width = 4 * ROWS
    centre = first / width
    reciprocal = lax.rsqrt(second / width - centre * centre + EPSILON)
    gain = ng_ref[...].astype(F32)
    centred = (x_ref[0].astype(F32) - centre) * reciprocal
    buf.centred[...] = centred
    buf.recip[...] = jnp.broadcast_to(reciprocal, (SEQ, HEAD))
    buf.norm[...] = (centred * gain).astype(BF16)
    near_step(*cs, down)
    near_step(*cs, across)
    own_send(buf.norm, buf.big_x, acts)
    gain_rows = jnp.zeros((8, QKV), F32)
    for j in range(4):
        row = stat_a.slots[4 * d + j, :, SEQ:].astype(BF16)
        gain_rows = gain_rows + dot(row, w[j * FEATURES : (j + 1) * FEATURES, 0:QKV])
    sums.out[...] = gain_rows
    small_start(sums)
    near_step(*cs, up)
    side_step(*cs, down)
    side_step(*cs, across)
    near_step(*cs, d)
    side_step(*cs, up)
    far_step(*cs, across)
    near_step(*xs, across)
    multiply_step(*cs, *cw, 2)
    near_step(*xs, up)
    side_step(*xs, across)
    far_step(*cs, up)
    near_step(*xs, down)
    far_step(*cs, down)
    near_step(*xs, d)
    far_step(*xs, across)
    multiply_step(*cs, *cw, 3)
    multiply_step(*xs, *xw, 2)
    side_step(*xs, down)
    side_step(*cs, d)
    side_sent(*xs, up)
    multiply_step(*cs, *cw, 1)
    side_step(*xs, d)
    side_step(*xs, up)
    far_step(*cs, d)
    far_step(*xs, up)
    far_step(*xs, down)
    multiply_step(*xs, *xw, 3)
    side_sent(*cs, down)
    pass_on(cots, *cw, 0, 0)
    multiply_step(*xs, *xw, 1)
    multiply_step(*cs, *cw, 0)
    far_step(*xs, d)
    pass_on(acts, *xw, 1, 1)
    pass_on(cots, *cw, 1, 1)
    multiply_step(*xs, *xw, 0)
    pass_on(acts, *xw, 0, 0)
    finish_depth(acts, *xw)
    own = buf.own_acc
    for h in range(2):
        cols = [slice(part * 256 + h * HEAD, part * 256 + (h + 1) * HEAD) for part in range(4)]
        for part in range(2):
            hat, rec = normalize(own[:, cols[part]])
            buf.hats[2 * part + h] = hat
            buf.recs[2 * part + h] = jnp.broadcast_to(rec, (SEQ, HEAD))
            row = hg_ref[0, part, h : h + 1, :].astype(F32)
            buf.lows[2 * part + h] = (hat * row).astype(BF16)
        buf.lows[4 + h] = own[:, cols[2]].astype(BF16)
        scores = dot_nt(buf.lows[h], buf.lows[2 + h]) * SCALE
        exponent = jnp.exp(scores)
        attention = exponent / jnp.sum(exponent, axis=-1, keepdims=True)
        buf.attention[h] = attention
        attended = dot(attention.astype(BF16), buf.lows[4 + h])
        buf.att[tokens(d), h * HEAD : (h + 1) * HEAD] = attended.astype(BF16)
    ring_start(buf.att, cots)
    ring_more(buf.att, cots)
    finish_depth(cots, *cw)
    gains.out[...] = jnp.zeros((8, HEAD), F32)
    gain_row = small_finish(sums)[0:1]
    firsts = jnp.zeros((SEQ, HEAD), F32)
    seconds = jnp.zeros((SEQ, HEAD), F32)
    for h in range(2):
        d_attended = own[:, QKV + h * HEAD : QKV + (h + 1) * HEAD].astype(BF16)
        attention = buf.attention[h]
        d_attention = dot_nt(d_attended, buf.lows[4 + h])
        row_delta = jnp.sum(attention * d_attention, axis=-1, keepdims=True)
        d_score = (attention * (d_attention - row_delta) * SCALE).astype(BF16)
        d_query = dot(d_score, buf.lows[2 + h])
        d_key = dot_tn(d_score, buf.lows[h])
        d_value = dot_tn(attention.astype(BF16), d_attended)
        for part, upstream in enumerate((d_query, d_key)):
            hat = buf.hats[2 * part + h]
            row = hg_ref[0, part, h : h + 1, :].astype(F32)
            grad = normalize_back(upstream, hat, buf.recs[2 * part + h][:, 0:1], row)
            at_col = part * 256 + h * HEAD
            low = grad.astype(BF16)
            buf.dp[tokens(d), at_col : at_col + HEAD] = low
            firsts = firsts + low.astype(F32) * gain_row[:, at_col : at_col + HEAD]
            seconds = seconds + low.astype(F32) * own[:, at_col : at_col + HEAD]
            index = 2 * part + h
            gains.out[index : index + 1, :] = jnp.sum(upstream * hat, axis=0, keepdims=True)
        at_col = 512 + h * HEAD
        low = d_value.astype(BF16)
        buf.dp[tokens(d), at_col : at_col + HEAD] = low
        firsts = firsts + low.astype(F32) * gain_row[:, at_col : at_col + HEAD]
        seconds = seconds + low.astype(F32) * own[:, at_col : at_col + HEAD]
    small_start(gains)
    first_stage(buf.att, branch, QKV, d)
    ring_start(buf.dp, acts)
    stat_start(
        stat_b,
        jnp.sum(firsts, axis=-1, keepdims=True),
        jnp.sum(seconds, axis=-1, keepdims=True),
    )
    second_stage(branch, d)
    ring_forward(buf.att, cots)
    first_stage(buf.dp, inputs, 0, d)
    ring_near(buf.att, cots)
    first_stage(buf.att, branch, QKV, down)
    first_stage(buf.att, branch, QKV, up)
    second_stage(branch, down)
    ring_more(buf.dp, acts)
    second_stage(branch, up)
    third_stage(branch, down)
    third_stage(branch, up)
    ring_far(buf.att, cots)
    side_sent(*xs, across)
    second_stage(inputs, d)
    third_stage(branch, d)
    first_stage(buf.att, branch, QKV, across)
    fourth_stage(branch, down)
    side_sent(*xs, down)
    side_done(branch, up)
    ring_forward(buf.dp, acts)
    ring_near(buf.dp, acts)
    second_stage(branch, across)
    side_done(branch, d)
    fourth_stage(branch, up)
    first_stage(buf.dp, inputs, 0, up)
    third_stage(inputs, d)
    weight_out(5)
    third_stage(branch, across)
    second_stage(inputs, up)
    first_stage(buf.dp, inputs, 0, down)
    fifth_stage(branch, up)
    fifth_stage(branch, down)
    side_sent(*cs, up)
    second_stage(inputs, down)
    fourth_stage(branch, d)
    weight_out(1)
    third_stage(inputs, up)
    third_stage(inputs, down)
    weight_out(4)
    ring_far(buf.dp, acts)
    first_stage(buf.dp, inputs, 0, across)
    second_stage(inputs, across)
    side_sent(*xs, d)
    side_done(inputs, down)
    fourth_stage(branch, across)
    fifth_stage(branch, d)
    weight_qkv(2)
    fourth_stage(inputs, down)
    side_done(inputs, up)
    weight_qkv(1)
    side_sent(*cs, across)
    third_stage(inputs, across)
    weight_qkv(0)
    weight_out(0)
    weight_out(3)
    side_done(inputs, d)
    fourth_stage(inputs, up)
    weight_qkv(5)
    side_sent(*cs, d)
    weight_qkv(3)
    side_done(inputs, across)
    side_done(branch, down)
    fourth_stage(inputs, d)
    fourth_stage(inputs, across)
    weight_qkv(4)
    first, second = stat_finish(stat_b)
    reciprocal = buf.recip[:, 0:1]
    centred = buf.centred[...]
    d_normed = last_stage(inputs)
    weighted = d_normed * gain
    grad = reciprocal * (weighted - first / width - centred * (second / width))
    buf.grad_out[...] = grad.astype(BF16)
    grad_copy = remote(
        buf.grad_out,
        buf.grad_in,
        sems.grad_send.at[0],
        sems.grad_recv.at[0],
        (section_down, d, g),
    )
    grad_copy.start()
    norms.out[...] = jnp.broadcast_to(
        jnp.sum(d_normed * centred, axis=0, keepdims=True), (8, FEATURES)
    )
    small_start(norms)
    total = small_finish(gains)
    for part in range(2):
        hgg_ref[0, part] = total[2 * part : 2 * part + 2]
    drain_gather(cot_ref.at[0], buf.big_c, cots)
    drain_gather(buf.norm, buf.big_x, acts)
    drain_depth(acts, 0, QKV)
    drain_depth(cots, QKV, 256)
    for step in range(4, 6):
        ring_copy(buf.att, cots, step).wait_send()
        ring_copy(buf.dp, acts, step).wait_send()
    fifth_stage(branch, across)
    side_done(branch, across)
    weight_out(2)
    nb_ref[0] = last_stage(branch).astype(BF16)
    drain_reduce(branch)
    drain_reduce(inputs)
    stat_drain(stat_a)
    stat_drain(stat_b)
    small_drain(gains)
    small_drain(sums)
    small_drain(norms)
    ngg_ref[...] = small_finish(norms)[0:1]
    grad_copy.wait()
    rg_ref[0] = buf.grad_in[...]


def local(section_input, cotangent, projections, norm_gain, head_gains):
    here = pl.BlockSpec(memory_space=pltpu.VMEM)
    outs = pl.pallas_call(
        kernel,
        out_shape=(
            jax.ShapeDtypeStruct((1, SEQ, FEATURES), BF16),
            jax.ShapeDtypeStruct((1, SEQ, FEATURES), BF16),
            jax.ShapeDtypeStruct((ROWS, COLS), BF16),
            jax.ShapeDtypeStruct((1, FEATURES), F32),
            jax.ShapeDtypeStruct((1, 2, 2, HEAD), F32),
        ),
        in_specs=[here, here, pl.BlockSpec(memory_space=pl.ANY), here, here],
        out_specs=(here,) * 5,
        scratch_shapes=LEAVES,
        compiler_params=pltpu.CompilerParams(
            collective_id=0, has_side_effects=True, vmem_limit_bytes=60 * 1024 * 1024
        ),
        name="block",
    )(section_input, cotangent, projections, norm_gain, head_gains)
    next_branch, returned, weight_grad, norm_total, head_total = outs
    return (
        next_branch,
        returned,
        weight_grad.reshape(1, ROWS, 4, 256),
        norm_total,
        head_total,
    )


def solution(mesh):
    in_specs = (
        P("section", "depth", "grid"),
        P("section", "depth", "grid"),
        P("section", "depth", None, "grid"),
        P("section", "grid"),
        P("section", None, "grid", None),
    )
    out_specs = (
        P("section", "depth", "grid"),
        P("section", "depth", "grid"),
        P("section", "depth", None, "grid"),
        P("section", "grid"),
        P("section", None, "grid", None),
    )
    return jax.shard_map(local, mesh=mesh, in_specs=in_specs, out_specs=out_specs, check_vma=False)
```

```python
from types import SimpleNamespace

import jax
import jax.numpy as jnp
from jax import lax
from jax.experimental import pallas as pl
from jax.experimental.pallas import tpu as pltpu
from jax.sharding import PartitionSpec as P

SEQ = 256
HALF = 128
QUARTER = 64
EPSILON = 1e-06
MESH = pl.DeviceIdType.MESH
BF16 = jnp.bfloat16
F32 = jnp.float32
FEATURES = 384
ROWS = 1536
HEAD = 128
QKV = 768
COLS = 1024
GRID = 16
SCALE = HEAD ** (-0.5)


def remote(src, dst, send_sem, recv_sem, device):
    return pltpu.make_async_remote_copy(
        src_ref=src,
        dst_ref=dst,
        send_sem=send_sem,
        recv_sem=recv_sem,
        device_id=device,
        device_id_type=MESH,
    )


def normalize(values):
    centre = jnp.mean(values, axis=-1, keepdims=True)
    second = jnp.mean(values * values, axis=-1, keepdims=True)
    reciprocal = lax.rsqrt(second - centre * centre + EPSILON)
    return (values - centre) * reciprocal, reciprocal


def normalize_back(upstream, normed, reciprocal, gain_row):
    scaled = upstream * gain_row
    first_mean = jnp.mean(scaled, axis=-1, keepdims=True)
    second_mean = jnp.mean(scaled * normed, axis=-1, keepdims=True)
    return reciprocal * (scaled - first_mean - normed * second_mean)


def dot(a, b):
    return jnp.dot(a, b, preferred_element_type=F32)


def dot_nt(a, b):
    return lax.dot_general(a, b, (((1,), (1,)), ((), ())), preferred_element_type=F32)


def dot_tn(a, b):
    return lax.dot_general(a, b, (((0,), (0,)), ((), ())), preferred_element_type=F32)


def vmem(shape, dtype):
    return pltpu.VMEM(shape, dtype)


def dma(count):
    return pltpu.SemaphoreType.DMA((count,))


def gather_scratch():
    return dict(
        own_send=dma(4),
        near_recv=dma(4),
        side_send=dma(8),
        side_recv=dma(8),
        far_send=dma(8),
        far_recv=dma(8),
        sib_send=dma(16),
        sib_recv=dma(16),
        half_send=dma(2),
        half_recv=dma(2),
        full_send=dma(4),
        full_recv=dma(4),
        ring_send=dma(6),
        ring_recv=dma(6),
    )


def reduce_scratch():
    return dict(
        sib_out=vmem((8, SEQ, FEATURES), BF16),
        sib_in=vmem((8, SEQ, FEATURES), BF16),
        keep=vmem((8, SEQ, FEATURES), F32),
        far_out=vmem((8, QUARTER, FEATURES), BF16),
        far_in=vmem((8, QUARTER, FEATURES), BF16),
        side_out=vmem((8, HALF, FEATURES), BF16),
        side_in=vmem((8, HALF, FEATURES), BF16),
        total=vmem((4, HALF, FEATURES), F32),
        next_out=vmem((4, HALF, FEATURES), BF16),
        mate_in=vmem((4, HALF, FEATURES), BF16),
        last_in=vmem((4, HALF, FEATURES), BF16),
        r_sib_send=dma(8),
        r_sib_recv=dma(8),
        r_far_send=dma(8),
        r_far_recv=dma(8),
        r_side_send=dma(8),
        r_side_recv=dma(8),
        r_next_send=dma(4),
        r_mate_recv=dma(4),
        r_last_recv=dma(4),
    )


def sum_scratch(count, rows, columns):
    return dict(
        out=vmem((rows, columns), F32),
        slots=vmem((count, rows, columns), F32),
        send=dma(count),
        recv=dma(count),
    )


SCRATCH = dict(
    acts=gather_scratch(),
    cots=gather_scratch(),
    branch=reduce_scratch(),
    inputs=reduce_scratch(),
    stat_a=sum_scratch(GRID, 8, SEQ + FEATURES),
    sums=sum_scratch(4, 8, QKV),
    stat_b=sum_scratch(GRID, 8, SEQ),
    gains=sum_scratch(4, 8, HEAD),
    norms=sum_scratch(4, 8, FEATURES),
    sems=dict(w=dma(1), grad_send=dma(1), grad_recv=dma(1)),
    buf=dict(
        w=vmem((ROWS, COLS), BF16),
        raw=vmem((ROWS, 4, 256), BF16),
        norm=vmem((SEQ, FEATURES), BF16),
        centred=vmem((SEQ, FEATURES), F32),
        recip=vmem((SEQ, HEAD), F32),
        big_x=vmem((4 * SEQ, ROWS), BF16),
        big_c=vmem((4 * SEQ, ROWS), BF16),
        far_out=vmem((SEQ, COLS), BF16),
        up_out=vmem((SEQ, COLS), BF16),
        down_out=vmem((SEQ, COLS), BF16),
        half_minus=vmem((SEQ, COLS), BF16),
        half_plus=vmem((SEQ, COLS), BF16),
        full_minus=vmem((SEQ, COLS), BF16),
        full_plus=vmem((SEQ, COLS), BF16),
        up_acc=vmem((SEQ, COLS), F32),
        down_acc=vmem((SEQ, COLS), F32),
        own_acc=vmem((SEQ, COLS), F32),
        attention=vmem((2, SEQ, SEQ), F32),
        hats=vmem((4, SEQ, HEAD), F32),
        recs=vmem((4, SEQ, HEAD), F32),
        lows=vmem((6, SEQ, HEAD), BF16),
        att=vmem((4 * SEQ, 256), BF16),
        dp=vmem((4 * SEQ, QKV), BF16),
        grad_out=vmem((SEQ, FEATURES), BF16),
        grad_in=vmem((SEQ, FEATURES), BF16),
    ),
)
LEAVES, TREE = jax.tree.flatten(SCRATCH)


def kernel(*refs):
    x_ref, cot_ref, w_hbm, ng_ref, hg_ref = refs[:5]
    nb_ref, rg_ref, dw_ref, ngg_ref, hgg_ref = refs[5:10]
    parts = jax.tree.unflatten(TREE, refs[10:])
    parts = {name: SimpleNamespace(**part) for name, part in parts.items()}
    acts, cots, branch, inputs = (parts[name] for name in ("acts", "cots", "branch", "inputs"))
    stat_a, stat_b = parts["stat_a"], parts["stat_b"]
    gains, norms, sums = parts["gains"], parts["norms"], parts["sums"]
    sems, buf = parts["sems"], parts["buf"]
    w = buf.w

    s = lax.axis_index("section")
    d = lax.axis_index("depth")
    g = lax.axis_index("grid")
    z = g // 8
    x = (g // 2) % 4
    c = g % 2
    base = 2 * (d % 2)
    place = (x - base + 4) % 4
    up = (d + 1) % 4
    down = (d + 3) % 4
    across = (d + 2) % 4

    def at(depth, z_, x_, c_, section=None):
        return (s if section is None else section, depth, z_ * 8 + x_ * 2 + c_)

    sibling = at(d, z, x, 1 - c)
    left_x = (x + 3) % 4
    right_x = (x + 1) % 4
    places = (x, left_x, right_x, (x + 2) % 4)
    left = at(d, z, left_x, c)
    right = at(d, z, right_x, c)
    above = at(up, z, x, c)
    below = at(down, z, x, c)
    section_up = (s + 1) % 4
    section_down = (s + 3) % 4
    home = g // 4
    home_block = g % 4
    home_base = 2 * (home % 2)
    home_other = (home_base + 3 - (x - home_base + 4) % 4) % 4
    owner_x = base + ((place + 1) // 2) % 2
    mate = at(d, 1 - z, x, c)

    def entry(t, depth):
        k = (t - depth + 4) % 4
        middle = depth // 2
        return (k % 2) * ((3 - k) // 2) + (1 - k % 2) * (middle + (k // 2) * (1 - 2 * middle))


    barrier = pltpu.get_barrier_semaphore()

    def greet(device):
        pl.semaphore_signal(barrier, inc=1, device_id=device, device_id_type=MESH)

    for k in range(1, GRID):
        greet((s, d, (g + k) % GRID))
    for k in range(1, 4):
        greet(at((d + k) % 4, z, x, c))
        greet(at((d + k) % 4, d // 2, owner_x, c))
    greet((section_up, d, g))
    for zz in range(2):
        for xx in (x, home_other):
            greet(at(home, zz, xx, c, section_down))

    @pl.when(home != d)
    def _():
        for zz in range(2):
            for xx in (x, home_other):
                greet(at(home, zz, xx, c))

    pl.semaphore_wait(barrier, 26 + 4 * (((home - d + 4) % 4 + 3) // 4))

    w_copy = pltpu.make_async_copy(w_hbm.at[0], buf.raw, sems.w.at[0])
    w_copy.start()

    def tokens(t):
        return pl.ds(pl.multiple_of(t * SEQ, SEQ), SEQ)

    def features(j):
        return pl.ds(pl.multiple_of(j * FEATURES, FEATURES), FEATURES)

    def own_copy(src, big, kind, h, zz):
        rows = pl.ds(pl.multiple_of(d * SEQ + h * HALF, HALF), HALF)
        return remote(
            src.at[h * HALF : (h + 1) * HALF, :],
            big.at[rows, features(home_block)],
            kind.own_send.at[2 * h + zz],
            kind.near_recv.at[d],
            at(home, zz, home_other if h else x, c),
        )

    def own_send(src, big, kind):
        for zz in range(2):
            here = jnp.logical_and(home == d, z == zz)

            @pl.when(here)
            def _():
                pltpu.make_async_copy(
                    src.at[0:HALF, :],
                    big.at[pl.ds(pl.multiple_of(d * SEQ, SEQ), HALF), features(home_block)],
                    kind.near_recv.at[d],
                ).start()

            @pl.when(jnp.logical_not(here))
            def _():
                own_copy(src, big, kind, 0, zz).start()

            own_copy(src, big, kind, 1, zz).start()

    def block(big, t, x_, c_, lo=0, count=HALF):
        p = (x_ - base + 4) % 4
        start = pl.multiple_of(t * SEQ + (p // 2) * HALF + lo, QUARTER)
        return big.at[pl.ds(start, count), features(2 * (((p + 1) // 2) % 2) + c_)]

    def side_copy(big, kind, t, side, arriving=False):
        ref = block(big, t, places[1 + side] if arriving else x, c)
        slot = 2 * t + side
        return remote(
            ref, ref, kind.side_send.at[slot], kind.side_recv.at[slot], (right, left)[side]
        )

    def far_copy(big, kind, t, side, arriving=False):
        ref = block(big, t, places[3 if arriving else 1 + side], c, side * QUARTER, QUARTER)
        slot = 2 * t + side
        return remote(
            ref, ref, kind.far_send.at[slot], kind.far_recv.at[slot], (right, left)[side]
        )

    def sib_copy(big, kind, t, part, arriving=False):
        ref = block(big, t, places[part], 1 - c if arriving else c)
        slot = 4 * t + part
        return remote(ref, ref, kind.sib_send.at[slot], kind.sib_recv.at[slot], sibling)

    def near_step(big, kind, t):
        ref = block(big, t, x, c)
        remote(ref, ref, kind.side_send.at[2 * t], kind.near_recv.at[t], right).wait_recv()
        side_copy(big, kind, t, 0).start()
        side_copy(big, kind, t, 1).start()
        sib_copy(big, kind, t, 0).start()

    def side_sent(big, kind, t):
        side_copy(big, kind, t, 0).wait_send()
        side_copy(big, kind, t, 1).wait_send()

    def side_step(big, kind, t):
        for side in range(2):
            side_copy(big, kind, t, side, True).wait_recv()
            far_copy(big, kind, t, side).start()
            sib_copy(big, kind, t, 1 + side).start()

    def far_step(big, kind, t):
        far_copy(big, kind, t, 0, True).wait_recv()
        far_copy(big, kind, t, 1, True).wait_recv()
        sib_copy(big, kind, t, 3).start()

    def sib_step(big, kind, t):
        for part in range(4):
            sib_copy(big, kind, t, part, True).wait_recv()

    def drain_gather(src, big, kind):
        for zz in range(2):

            @pl.when(jnp.logical_or(home != d, z != zz))
            def _():
                own_copy(src, big, kind, 0, zz).wait_send()

            own_copy(src, big, kind, 1, zz).wait_send()
        for t in range(4):
            for part in range(4):
                sib_copy(big, kind, t, part).wait_send()
            far_copy(big, kind, t, 0).wait_send()
            far_copy(big, kind, t, 1).wait_send()

    def half_copy(kind, lo, count, side):
        cut = lo + side * (count // 2)
        cols = slice(cut, cut + count // 2)
        dst = buf.half_minus if side == 0 else buf.half_plus
        return remote(
            buf.far_out.at[:, cols],
            dst.at[:, cols],
            kind.half_send.at[side],
            kind.half_recv.at[side],
            above if side == 0 else below,
        )

    def full_copy(kind, lo, count, side, part):
        cut = lo + part * (count // 2)
        cols = slice(cut, cut + count // 2)
        src = buf.up_out if side == 0 else buf.down_out
        dst = buf.full_minus if side == 0 else buf.full_plus
        return remote(
            src.at[:, cols],
            dst.at[:, cols],
            kind.full_send.at[2 * side + part],
            kind.full_recv.at[2 * side + part],
            above if side == 0 else below,
        )

    def pass_on(kind, lo, count, side, part):
        acc = buf.up_acc if side == 0 else buf.down_acc
        out = buf.up_out if side == 0 else buf.down_out
        got = buf.half_minus if side == 0 else buf.half_plus
        cut = lo + part * (count // 2)
        cols = slice(cut, cut + count // 2)
        value = acc[:, cols]
        if part == side:
            half_copy(kind, lo, count, side).wait_recv()
            value = value + got[:, cols].astype(F32)
        out[:, cols] = value.astype(BF16)
        full_copy(kind, lo, count, side, part).start()

    def multiply(big, kind, lo, count, t, ref):
        sib_step(big, kind, t)
        for q in range(lo, lo + count, 256):
            ref[:, q : q + 256] = dot(big[tokens(t), :], w[:, q : q + 256]).astype(ref.dtype)

    def multiply_step(big, kind, lo, count, r):
        if r == 0:
            multiply(big, kind, lo, count, d, buf.own_acc)
        elif r == 1:
            multiply(big, kind, lo, count, up, buf.up_acc)
            pass_on(kind, lo, count, 0, 1)
        elif r == 3:
            multiply(big, kind, lo, count, down, buf.down_acc)
            pass_on(kind, lo, count, 1, 0)
        else:
            multiply(big, kind, lo, count, across, buf.far_out)
            half_copy(kind, lo, count, 0).start()
            half_copy(kind, lo, count, 1).start()

    def finish_depth(kind, lo, count):
        cols = slice(lo, lo + count)
        for side in range(2):
            full_copy(kind, lo, count, side, 0).wait_recv()
            full_copy(kind, lo, count, side, 1).wait_recv()
        buf.own_acc[:, cols] = (
            buf.own_acc[:, cols]
            + buf.full_minus[:, cols].astype(F32)
            + buf.full_plus[:, cols].astype(F32)
        )

    def drain_depth(kind, lo, count):
        for side in range(2):
            half_copy(kind, lo, count, side).wait_send()
            full_copy(kind, lo, count, side, 0).wait_send()
            full_copy(kind, lo, count, side, 1).wait_send()

    def ring_block(ref, step, t):
        half = ref.shape[1] // 2
        second = step in (1, 2, 5)
        return ref.at[tokens(t), half:] if second else ref.at[tokens(t), :half]

    def ring_copy(ref, kind, step):
        block = ring_block(ref, step, (d, d, d, d, down, up)[step])
        return remote(
            block,
            block,
            kind.ring_send.at[step],
            kind.ring_recv.at[step],
            above if step % 2 == 0 else below,
        )

    def ring_wait(ref, kind, step):
        block = ring_block(ref, step, (down, up, down, up, across, across)[step])
        remote(
            block,
            block,
            kind.ring_send.at[step],
            kind.ring_recv.at[step],
            above if step % 2 == 0 else below,
        ).wait_recv()

    def ring_start(ref, kind):
        ring_copy(ref, kind, 0).start()
        ring_copy(ref, kind, 1).start()

    def ring_more(ref, kind):
        for step in range(2):
            ring_copy(ref, kind, step).wait_send()
            ring_copy(ref, kind, step + 2).start()

    def ring_forward(ref, kind):
        for step in range(2):
            ring_wait(ref, kind, step)
            ring_copy(ref, kind, step + 2).wait_send()
            ring_copy(ref, kind, step + 4).start()

    def ring_near(ref, kind):
        ring_wait(ref, kind, 2)
        ring_wait(ref, kind, 3)

    def ring_far(ref, kind):
        ring_wait(ref, kind, 4)
        ring_wait(ref, kind, 5)

    def r_sib(kind, t, i):
        slot = 2 * t + i
        return remote(
            kind.sib_out.at[slot],
            kind.sib_in.at[slot],
            kind.r_sib_send.at[slot],
            kind.r_sib_recv.at[slot],
            sibling,
        )

    def r_far(kind, t, side):
        slot = 2 * t + side
        return remote(
            kind.far_out.at[slot],
            kind.far_in.at[slot],
            kind.r_far_send.at[slot],
            kind.r_far_recv.at[slot],
            (right, left)[side],
        )

    def r_side(kind, t, side):
        slot = 2 * t + side
        return remote(
            kind.side_out.at[slot],
            kind.side_in.at[slot],
            kind.r_side_send.at[slot],
            kind.r_side_recv.at[slot],
            (right, left)[side],
        )

    def r_mate(kind, t):
        return remote(
            kind.next_out.at[t],
            kind.mate_in.at[t],
            kind.r_next_send.at[t],
            kind.r_mate_recv.at[t],
            mate,
        )

    def r_last(kind, t, act):
        slot = place // 2 if kind is branch else 2 * (place // 2) + z
        dst = kind.last_in.at[slot]
        recv = kind.r_last_recv.at[slot]
        src = kind.next_out.at[t]
        section = section_up if kind is branch else s
        copy = remote(src, dst, kind.r_next_send.at[t], recv, at(t, d // 2, owner_x, c, section))

        def away():
            if act == "start":
                copy.start()
            else:
                copy.wait_send()

        if kind is branch:
            away()
        else:
            here = jnp.logical_and(t == d, jnp.logical_and(place < 2, z == d // 2))
            pl.when(jnp.logical_not(here))(away)

            @pl.when(here)
            def _():
                if act == "start":
                    pltpu.make_async_copy(src, dst, recv).start()

    def total_of(kind, t, x_, lo, count):
        p = (x_ - base + 4) % 4
        slot = 2 * t + ((p + 1) // 2) % 2
        rows = pl.ds(pl.multiple_of((p // 2) * HALF + lo, QUARTER), count)
        return kind.keep[slot, rows, :] + kind.sib_in[slot, rows, :].astype(F32)

    def first_stage(ref, kind, lo, t):
        count = ref.shape[1]
        left = ref[tokens(t), :]
        for i in range(2):
            rows = features(2 * i + 1 - c)
            value = dot_nt(left, w[rows, lo : lo + count])
            kind.sib_out[2 * t + i] = value.astype(BF16)
            r_sib(kind, t, i).start()
        for i in range(2):
            rows = features(2 * i + c)
            kind.keep[2 * t + i] = dot_nt(left, w[rows, lo : lo + count])

    def second_stage(kind, t):
        r_sib(kind, t, 0).wait_recv()
        r_sib(kind, t, 1).wait_recv()
        for side in range(2):
            value = total_of(kind, t, places[3], side * QUARTER, QUARTER)
            kind.far_out[2 * t + side] = value.astype(BF16)
            r_far(kind, t, side).start()

    def third_stage(kind, t):
        for side in range(2):
            slot = 2 * t + side
            r_far(kind, t, side).wait_recv()
            for part in range(2):
                value = total_of(kind, t, places[2 - side], part * QUARTER, QUARTER)
                if part == side:
                    value = value + kind.far_in[slot].astype(F32)
                kind.side_out[slot, part * QUARTER : (part + 1) * QUARTER, :] = value.astype(BF16)
            r_side(kind, t, side).start()

    def side_done(kind, t):
        r_side(kind, t, 0).wait_send()
        r_side(kind, t, 1).wait_send()

    def fourth_stage(kind, t):
        r_side(kind, t, 0).wait_recv()
        r_side(kind, t, 1).wait_recv()
        total = total_of(kind, t, x, 0, HALF)
        total = total + kind.side_in[2 * t].astype(F32) + kind.side_in[2 * t + 1].astype(F32)
        if kind is inputs:
            kind.next_out[t] = total.astype(BF16)
            r_last(kind, t, "start")
            return
        kind.total[t] = total

        @pl.when(z != entry(t, d))
        def _():
            kind.next_out[t] = total.astype(BF16)
            r_mate(kind, t).start()

    def fifth_stage(kind, t):
        @pl.when(z == entry(t, d))
        def _():
            r_mate(kind, t).wait_recv()
            total = kind.total[t] + kind.mate_in[t].astype(F32)
            kind.next_out[t] = total.astype(BF16)
            r_last(kind, t, "start")

    def last_stage(kind):
        count = 2 if kind is branch else 4
        for slot in range(count):
            remote(
                kind.last_in.at[slot],
                kind.last_in.at[slot],
                kind.r_next_send.at[0],
                kind.r_last_recv.at[slot],
                sibling,
            ).wait_recv()
        if kind is branch:
            return kind.last_in[0:2].reshape(SEQ, FEATURES).astype(F32)
        halves = [
            kind.last_in[2 * h].astype(F32) + kind.last_in[2 * h + 1].astype(F32) for h in range(2)
        ]
        return jnp.concatenate(halves, axis=0)

    def drain_reduce(kind):
        for t in range(4):
            r_sib(kind, t, 0).wait_send()
            r_sib(kind, t, 1).wait_send()
            r_far(kind, t, 0).wait_send()
            r_far(kind, t, 1).wait_send()

            if kind is inputs:
                r_last(kind, t, "wait")
                continue

            @pl.when(z != entry(t, d))
            def _():
                r_mate(kind, t).wait_send()

            @pl.when(z == entry(t, d))
            def _():
                r_last(kind, t, "wait")

    def stat_copy(name, k):
        return remote(
            name.out,
            name.slots.at[g],
            name.send.at[k],
            name.recv.at[k],
            (s, d, (g + k) % GRID),
        )

    lane = lax.broadcasted_iota(jnp.int32, (SEQ, HEAD), 1)

    def stat_start(name, first, second):
        both = jnp.where(lane == 0, first, jnp.where(lane == 1, second, 0.0))
        turned = both.T[0:8]
        name.out[:, 0:SEQ] = turned
        if name is stat_a:
            name.out[:, SEQ:] = jnp.broadcast_to(ng_ref[...].astype(F32), (8, FEATURES))
        name.slots[g] = name.out[...]
        for k in range(1, GRID):
            stat_copy(name, k).start()

    def stat_finish(name):
        slots = name.slots
        for k in range(1, GRID):
            slot = slots.at[(g + GRID - k) % GRID]
            remote(
                slot, slot, name.send.at[k], name.recv.at[k], sibling
            ).wait_recv()
        total = jnp.sum(slots[:, :, 0:SEQ], axis=0)
        padded = jnp.concatenate([total, jnp.zeros((HEAD - 8, SEQ), F32)], axis=0)
        columns = padded.T
        return columns[:, 0:1], columns[:, 1:2]

    def stat_drain(name):
        for k in range(1, GRID):
            stat_copy(name, k).wait_send()

    def small_copy(name, k):
        return remote(
            name.out,
            name.slots.at[d],
            name.send.at[k],
            name.recv.at[k],
            at((d + k) % 4, z, x, c),
        )

    def small_start(name):
        name.slots[d] = name.out[...]
        for k in range(1, 4):
            small_copy(name, k).start()

    def small_finish(name):
        slots = name.slots
        for k in range(1, 4):
            slot = slots.at[(d + 4 - k) % 4]
            remote(
                slot, slot, name.send.at[k], name.recv.at[k], above
            ).wait_recv()
        return jnp.sum(slots[...], axis=0)

    def small_drain(name):
        for k in range(1, 4):
            small_copy(name, k).wait_send()

    xs = (buf.big_x, acts)
    cs = (buf.big_c, cots)
    xw = (0, QKV)
    cw = (QKV, 256)
    def weight_qkv(k):
        rows = slice(k * 256, (k + 1) * 256)
        dw_ref[rows, 0:QKV] = dot_tn(buf.big_x[:, rows], buf.dp[...]).astype(BF16)

    def weight_out(k):
        rows = slice(k * 256, (k + 1) * 256)
        dw_ref[rows, QKV:COLS] = dot_tn(buf.big_c[:, rows], buf.att[...]).astype(BF16)

    def relayout(k, _):
        rows = pl.ds(pl.multiple_of(k * 128, 128), 128)
        chunk = buf.raw[rows]
        for part in range(4):
            w[rows, part * 256 : (part + 1) * 256] = chunk[:, part, :]
        return 0

    def relayout_all():
        w_copy.wait()
        lax.fori_loop(0, ROWS // 128, relayout, 0)

    own_send(cot_ref.at[0], buf.big_c, cots)
    values = x_ref[0].astype(F32)
    stat_start(
        stat_a,
        jnp.sum(values, axis=-1, keepdims=True),
        jnp.sum(values * values, axis=-1, keepdims=True),
    )
    relayout_all()
    first, second = stat_finish(stat_a)
    width = 4 * ROWS
    centre = first / width
    reciprocal = lax.rsqrt(second / width - centre * centre + EPSILON)
    gain = ng_ref[...].astype(F32)
    centred = (x_ref[0].astype(F32) - centre) * reciprocal
    buf.centred[...] = centred
    buf.recip[...] = jnp.broadcast_to(reciprocal, (SEQ, HEAD))
    buf.norm[...] = (centred * gain).astype(BF16)
    near_step(*cs, down)
    near_step(*cs, across)
    own_send(buf.norm, buf.big_x, acts)
    gain_rows = jnp.zeros((8, QKV), F32)
    for j in range(4):
        row = stat_a.slots[4 * d + j, :, SEQ:].astype(BF16)
        gain_rows = gain_rows + dot(row, w[j * FEATURES : (j + 1) * FEATURES, 0:QKV])
    sums.out[...] = gain_rows
    small_start(sums)
    near_step(*cs, up)
    side_step(*cs, down)
    side_step(*cs, across)
    near_step(*cs, d)
    side_step(*cs, up)
    far_step(*cs, across)
    near_step(*xs, across)
    multiply_step(*cs, *cw, 2)
    near_step(*xs, up)
    side_step(*xs, across)
    far_step(*cs, up)
    near_step(*xs, down)
    far_step(*cs, down)
    near_step(*xs, d)
    multiply_step(*cs, *cw, 1)
    far_step(*xs, across)
    multiply_step(*cs, *cw, 3)
    multiply_step(*xs, *xw, 2)
    side_step(*xs, down)
    side_sent(*xs, up)
    side_step(*cs, d)
    side_step(*xs, d)
    side_step(*xs, up)
    far_step(*cs, d)
    far_step(*xs, down)
    far_step(*xs, up)
    multiply_step(*xs, *xw, 3)
    pass_on(cots, *cw, 0, 0)
    multiply_step(*xs, *xw, 1)
    multiply_step(*cs, *cw, 0)
    pass_on(cots, *cw, 1, 1)
    far_step(*xs, d)
    pass_on(acts, *xw, 1, 1)
    multiply_step(*xs, *xw, 0)
    pass_on(acts, *xw, 0, 0)
    finish_depth(acts, *xw)
    own = buf.own_acc
    for h in range(2):
        cols = [slice(part * 256 + h * HEAD, part * 256 + (h + 1) * HEAD) for part in range(4)]
        for part in range(2):
            hat, rec = normalize(own[:, cols[part]])
            buf.hats[2 * part + h] = hat
            buf.recs[2 * part + h] = jnp.broadcast_to(rec, (SEQ, HEAD))
            row = hg_ref[0, part, h : h + 1, :].astype(F32)
            buf.lows[2 * part + h] = (hat * row).astype(BF16)
        buf.lows[4 + h] = own[:, cols[2]].astype(BF16)
        scores = dot_nt(buf.lows[h], buf.lows[2 + h]) * SCALE
        exponent = jnp.exp(scores)
        attention = exponent / jnp.sum(exponent, axis=-1, keepdims=True)
        buf.attention[h] = attention
        attended = dot(attention.astype(BF16), buf.lows[4 + h])
        buf.att[tokens(d), h * HEAD : (h + 1) * HEAD] = attended.astype(BF16)
    side_sent(*cs, down)
    ring_start(buf.att, cots)
    ring_more(buf.att, cots)
    finish_depth(cots, *cw)
    gains.out[...] = jnp.zeros((8, HEAD), F32)
    gain_row = small_finish(sums)[0:1]
    firsts = jnp.zeros((SEQ, HEAD), F32)
    seconds = jnp.zeros((SEQ, HEAD), F32)
    for h in range(2):
        d_attended = own[:, QKV + h * HEAD : QKV + (h + 1) * HEAD].astype(BF16)
        attention = buf.attention[h]
        d_attention = dot_nt(d_attended, buf.lows[4 + h])
        row_delta = jnp.sum(attention * d_attention, axis=-1, keepdims=True)
        d_score = (attention * (d_attention - row_delta) * SCALE).astype(BF16)
        d_query = dot(d_score, buf.lows[2 + h])
        d_key = dot_tn(d_score, buf.lows[h])
        d_value = dot_tn(attention.astype(BF16), d_attended)
        for part, upstream in enumerate((d_query, d_key)):
            hat = buf.hats[2 * part + h]
            row = hg_ref[0, part, h : h + 1, :].astype(F32)
            grad = normalize_back(upstream, hat, buf.recs[2 * part + h][:, 0:1], row)
            at_col = part * 256 + h * HEAD
            low = grad.astype(BF16)
            buf.dp[tokens(d), at_col : at_col + HEAD] = low
            firsts = firsts + low.astype(F32) * gain_row[:, at_col : at_col + HEAD]
            seconds = seconds + low.astype(F32) * own[:, at_col : at_col + HEAD]
            index = 2 * part + h
            gains.out[index : index + 1, :] = jnp.sum(upstream * hat, axis=0, keepdims=True)
        at_col = 512 + h * HEAD
        low = d_value.astype(BF16)
        buf.dp[tokens(d), at_col : at_col + HEAD] = low
        firsts = firsts + low.astype(F32) * gain_row[:, at_col : at_col + HEAD]
        seconds = seconds + low.astype(F32) * own[:, at_col : at_col + HEAD]
    small_start(gains)
    first_stage(buf.att, branch, QKV, d)
    ring_start(buf.dp, acts)
    second_stage(branch, d)
    stat_start(
        stat_b,
        jnp.sum(firsts, axis=-1, keepdims=True),
        jnp.sum(seconds, axis=-1, keepdims=True),
    )
    ring_forward(buf.att, cots)
    first_stage(buf.dp, inputs, 0, d)
    ring_near(buf.att, cots)
    first_stage(buf.att, branch, QKV, down)
    first_stage(buf.att, branch, QKV, up)
    second_stage(branch, down)
    ring_more(buf.dp, acts)
    second_stage(branch, up)
    third_stage(branch, down)
    third_stage(branch, up)
    ring_far(buf.att, cots)
    second_stage(inputs, d)
    third_stage(branch, d)
    side_sent(*xs, across)
    first_stage(buf.att, branch, QKV, across)
    fourth_stage(branch, down)
    weight_out(5)
    side_sent(*xs, down)
    side_done(branch, up)
    ring_forward(buf.dp, acts)
    ring_near(buf.dp, acts)
    second_stage(branch, across)
    side_done(branch, d)
    fourth_stage(branch, up)
    first_stage(buf.dp, inputs, 0, up)
    third_stage(inputs, d)
    third_stage(branch, across)
    second_stage(inputs, up)
    fifth_stage(branch, down)
    first_stage(buf.dp, inputs, 0, down)
    second_stage(inputs, down)
    fifth_stage(branch, up)
    side_sent(*cs, up)
    fourth_stage(branch, d)
    weight_out(1)
    third_stage(inputs, up)
    third_stage(inputs, down)
    weight_out(4)
    ring_far(buf.dp, acts)
    first_stage(buf.dp, inputs, 0, across)
    weight_qkv(2)
    second_stage(inputs, across)
    side_sent(*xs, d)
    side_done(inputs, down)
    fourth_stage(branch, across)
    fifth_stage(branch, d)
    fourth_stage(inputs, down)
    side_sent(*cs, across)
    side_done(inputs, up)
    weight_qkv(0)
    fourth_stage(inputs, up)
    weight_out(0)
    third_stage(inputs, across)
    weight_out(3)
    side_done(inputs, d)
    weight_qkv(1)
    weight_qkv(5)
    side_done(branch, down)
    side_sent(*cs, d)
    weight_qkv(3)
    side_done(inputs, across)
    fourth_stage(inputs, d)
    fourth_stage(inputs, across)
    weight_qkv(4)
    fifth_stage(branch, across)
    weight_out(2)
    side_done(branch, across)
    first, second = stat_finish(stat_b)
    reciprocal = buf.recip[:, 0:1]
    centred = buf.centred[...]
    d_normed = last_stage(inputs)
    weighted = d_normed * gain
    grad = reciprocal * (weighted - first / width - centred * (second / width))
    buf.grad_out[...] = grad.astype(BF16)
    grad_copy = remote(
        buf.grad_out,
        buf.grad_in,
        sems.grad_send.at[0],
        sems.grad_recv.at[0],
        (section_down, d, g),
    )
    grad_copy.start()
    norms.out[...] = jnp.broadcast_to(
        jnp.sum(d_normed * centred, axis=0, keepdims=True), (8, FEATURES)
    )
    small_start(norms)
    total = small_finish(gains)
    for part in range(2):
        hgg_ref[0, part] = total[2 * part : 2 * part + 2]
    nb_ref[0] = last_stage(branch).astype(BF16)
    drain_gather(cot_ref.at[0], buf.big_c, cots)
    drain_gather(buf.norm, buf.big_x, acts)
    drain_depth(acts, 0, QKV)
    drain_depth(cots, QKV, 256)
    for step in range(4, 6):
        ring_copy(buf.att, cots, step).wait_send()
        ring_copy(buf.dp, acts, step).wait_send()
    drain_reduce(branch)
    drain_reduce(inputs)
    stat_drain(stat_a)
    stat_drain(stat_b)
    small_drain(gains)
    small_drain(sums)
    small_drain(norms)
    ngg_ref[...] = small_finish(norms)[0:1]
    grad_copy.wait()
    rg_ref[0] = buf.grad_in[...]


def local(section_input, cotangent, projections, norm_gain, head_gains):
    here = pl.BlockSpec(memory_space=pltpu.VMEM)
    outs = pl.pallas_call(
        kernel,
        out_shape=(
            jax.ShapeDtypeStruct((1, SEQ, FEATURES), BF16),
            jax.ShapeDtypeStruct((1, SEQ, FEATURES), BF16),
            jax.ShapeDtypeStruct((ROWS, COLS), BF16),
            jax.ShapeDtypeStruct((1, FEATURES), F32),
            jax.ShapeDtypeStruct((1, 2, 2, HEAD), F32),
        ),
        in_specs=[here, here, pl.BlockSpec(memory_space=pl.ANY), here, here],
        out_specs=(here,) * 5,
        scratch_shapes=LEAVES,
        compiler_params=pltpu.CompilerParams(
            collective_id=0, has_side_effects=True, vmem_limit_bytes=60 * 1024 * 1024
        ),
        name="block",
    )(section_input, cotangent, projections, norm_gain, head_gains)
    next_branch, returned, weight_grad, norm_total, head_total = outs
    return (
        next_branch,
        returned,
        weight_grad.reshape(1, ROWS, 4, 256),
        norm_total,
        head_total,
    )


def solution(mesh):
    in_specs = (
        P("section", "depth", "grid"),
        P("section", "depth", "grid"),
        P("section", "depth", None, "grid"),
        P("section", "grid"),
        P("section", None, "grid", None),
    )
    out_specs = (
        P("section", "depth", "grid"),
        P("section", "depth", "grid"),
        P("section", "depth", None, "grid"),
        P("section", "grid"),
        P("section", None, "grid", None),
    )
    return jax.shard_map(local, mesh=mesh, in_specs=in_specs, out_specs=out_specs, check_vma=False)
```
